512 devices in a mesh: section: 16 (over x, y), expert: 32 (over z, core).
Axes of the slice: x: 4, y: 4, z: 16, core: 2. Of those that a mesh axis runs over, the one named last changes fastest.
Arguments:
- carried: bfloat16 [2, 16, 1536, 3584], P(None, 'section', 'expert'), may hold values from -6 to 6
- norm_gain: bfloat16 [16, 3584], P('section'), may hold values from 0.099609375 to 1.8984375
- router: bfloat16 [16, 3584, 8], P('section'), may hold values from -0.09375 to 0.09375
- w_up: bfloat16 [16, 3584, 8192], P('section', None, 'expert'), may hold values from -0.09375 to 0.09375
- w_down: bfloat16 [16, 8192, 3584], P('section', 'expert'), may hold values from -0.1875 to 0.1875
- expert_ids: int32 [16, 2, 1536, 1], P('section', None, 'expert'), may hold values from 0 to 7; in each aligned block of 48 rows (0 to 47, 48 to 95, ..., all dimensions but the last counted through in order) at most 9 rows name the same one
Outputs:
- advanced: bfloat16 [2, 16, 1536, 3584], P(None, 'section', 'expert')
The draws below stay inside these ranges and needn't reach their ends.
Inputs may be any that keep to these rules, and one draw needn't show every extreme that they name: `expert_ids`: within each aligned block of 48 tokens of one section and direction (the tokens of one device), at most 9 tokens choose any one expert, and some block reaches 9.
All inputs are finite; a program needn't handle non-finite values.
Results may differ from the reference program's by a relative error of at most 0.01.
Values may be sent and summed in bfloat16 or wider, within the bound.
No kernel may reach another device: no remote copies, remote signals or barrier semaphores. Data moves between devices by JAX's collectives and lax.ppermute only.
A program may use at most 64 MiB of HBM per device.

```python
import math
import jax
import jax.numpy as jnp
import numpy as np
from jax import lax

D = 3584
H = 1024
SPLIT = 4
TOP = 1
TOK_DEV = 48
HID_DEV = 256
EXPERTS = 8
CAP = 9
SECTIONS = 16
TOKENS = 1536


def shard_levels(stream_key, extent, split, least, high):
    loudness = 1.0
    for axis_at, shards_of in split:
        heights = jax.random.uniform(jax.random.fold_in(jax.random.fold_in(stream_key, 6), axis_at), (shards_of,), jnp.float32, least / len(split), high / len(split))
        loudness = loudness * jnp.repeat(jnp.exp(heights), extent[axis_at] // shards_of).reshape((-1,) + (1,) * (len(extent) - 1 - axis_at))
    return loudness


def shared_out(stream_key, own, number, rows, count, top, reach, skew):
    order = jax.random.permutation(stream_key, count)
    packed, common = shares(count, rows * top, reach, skew, True), shares(count, rows * top, reach, skew, False)
    places = jnp.arange(count)

    def named(sizes, turn):
        used = int((sizes > 0).sum())
        fixed = max(1, used // 4)
        moved = fixed + (places - fixed + turn * (used - fixed)) % max(1, count - fixed)
        return jnp.zeros((count,), jnp.int32).at[order[jnp.where(places < fixed, places, moved)]].set(jnp.asarray(sizes, jnp.int32))

    sizes = jnp.where(number % 4 == 0, named(packed, number // 4), named(common, number - number // 4 - 1))
    mixed = jax.random.permutation(jax.random.fold_in(own, 3), count)
    source_of, sink = mixed[0:count // 2 * 2:2], mixed[1:count // 2 * 2:2]
    slack = jnp.minimum(sizes[source_of] - 1, reach - sizes[sink]) // 2
    slack = jnp.where((source_of == order[0]) | (sink == order[0]) | (sizes[sink] == 0), 0, jnp.maximum(slack, 0))
    moved = jax.random.randint(jax.random.fold_in(own, 4), (count // 2,), 0, 1 << 20) % (slack + 1)
    sizes = sizes.at[source_of].add(-moved).at[sink].add(moved)
    items = jnp.searchsorted(jnp.cumsum(sizes), jnp.arange(rows * top), side="right").astype(jnp.int32)
    table = items.reshape(top, rows).T
    table = table[jax.random.permutation(jax.random.fold_in(own, 1), rows)]
    turn = jax.random.randint(jax.random.fold_in(own, 2), (rows, 1), 0, top)
    return jnp.take_along_axis(table, (jnp.arange(top)[None, :] + turn) % top, axis=1)


def shares(count, total, limit, slope, full):
    weights = [(1 << 20) // math.isqrt(standing ** slope) + 1 for standing in range(1, count + 1)]
    largest = limit if full else min(limit, max(-(-total // count), total * weights[0] // sum(weights)))
    least = 1 if total - largest >= count - 1 else 0
    given, rest = [largest] + [least] * (count - 1), total - largest - least * (count - 1)
    while rest > 0:
        movable = [i for i in range(1, count) if given[i] < largest] or [i for i in range(1, count) if given[i] < limit]
        whole, remaining = sum([weights[i] for i in movable]), rest
        for i in movable:
            more = min(limit - given[i], max(1, remaining * weights[i] // whole), rest)
            given[i] = given[i] + more
            rest = rest - more
    return np.array(given)


def normal_values(own_key, extent, scale, limit, cuts=(), held_as=jnp.bfloat16):
    values = jax.random.normal(own_key, extent, jnp.float32) * scale
    if len(cuts) > 0:
        values = shard_levels(own_key, extent, cuts, -0.22, 0.18) * values
    return jnp.clip(values, min=-limit, max=limit).astype(held_as)


def setup_inputs(seed: int = 0) -> dict:
    splits = jax.random.split(jax.random.key(seed), 7)
    carried = normal_values(splits[0], (2, SECTIONS, TOKENS, D), 1.0, 6.0, ((1, 16), (2, 32)))
    norm_gain = jnp.clip(1.0 + 0.18 * jax.random.normal(splits[1], (SECTIONS, D), jnp.float32), 0.099609375, 1.8984375).astype(jnp.bfloat16)
    router = normal_values(splits[2], (SECTIONS, D, EXPERTS), D ** -0.5, 0.09375, ((0, 16),))
    w_up = normal_values(splits[3], (SECTIONS, D, EXPERTS * H), D ** -0.5, 0.09375, ((0, 16), (2, 32)))
    w_down = normal_values(splits[4], (SECTIONS, EXPERTS * H, D), H ** -0.5, 0.1875, ((0, 16), (1, 32)))
    expert_ids_keys = jax.random.split(jax.random.fold_in(splits[5], 1), SECTIONS * 2 * TOKENS // TOK_DEV)
    expert_ids_turns = jax.random.permutation(jax.random.fold_in(splits[5], 3), SECTIONS * 2 * TOKENS // TOK_DEV)
    expert_ids = jax.vmap(lambda own, number: shared_out(jax.random.fold_in(splits[5], 2), own, number, TOK_DEV, EXPERTS, TOP, CAP, 2))(expert_ids_keys, expert_ids_turns).reshape((SECTIONS, 2, TOKENS, TOP))
    return dict(carried=carried, norm_gain=norm_gain, router=router, w_up=w_up, w_down=w_down, expert_ids=expert_ids)


epsilon = 1e-06
route_scale = 2.5

def normalize(activations, gain):
    widened = activations.astype(jnp.float32)
    mean_square = lax.optimization_barrier(jnp.mean(widened * widened, axis=-1, keepdims=True))
    return (widened * lax.rsqrt(mean_square + epsilon) * gain.astype(jnp.float32)).astype(jnp.bfloat16)

def moe_layer(activations, gain, router_matrix, up_matrix, down_matrix, chosen_ids):
    normed = normalize(activations, gain)
    logits = jnp.dot(normed, router_matrix, preferred_element_type=jnp.float32)
    chosen = chosen_ids[:, 0].astype(jnp.int32)
    one_hot = (chosen[:, None] == jnp.arange(EXPERTS, dtype=jnp.int32)[None, :]).astype(jnp.int32)
    gate_value = route_scale * jax.nn.sigmoid(lax.optimization_barrier(jnp.sum(logits * one_hot.astype(jnp.float32), axis=-1)))
    blocks = TOKENS // TOK_DEV
    block_hot = one_hot.reshape(blocks, TOK_DEV, EXPERTS)
    slot = lax.optimization_barrier(jnp.sum((jnp.cumsum(block_hot, axis=1) - block_hot) * block_hot, axis=-1))
    target = (chosen.reshape(blocks, TOK_DEV) * CAP + slot).astype(jnp.int32)
    block_ids = jnp.broadcast_to(jnp.arange(blocks, dtype=jnp.int32)[:, None], (blocks, TOK_DEV))
    slot_rows = jnp.zeros((blocks, EXPERTS * CAP, D), jnp.bfloat16).at[block_ids, target].set(normed.reshape(blocks, TOK_DEV, D))
    by_expert = slot_rows.reshape(blocks, EXPERTS, CAP, D).transpose(1, 0, 2, 3).reshape(EXPERTS, blocks * CAP, D)
    up_stack = up_matrix.reshape(D, EXPERTS, H).transpose(1, 0, 2)
    down_stack = down_matrix.reshape(EXPERTS, SPLIT, HID_DEV, D)

    def one_expert(operands):
        rows, up_part, down_part = operands
        hidden_pre = jnp.dot(rows, up_part, preferred_element_type=jnp.float32)
        activated = jax.nn.silu(hidden_pre).astype(jnp.bfloat16).reshape(rows.shape[0], SPLIT, HID_DEV)
        partial_value = jnp.einsum('rkh,khd->rkd', activated.astype(jnp.float32), down_part.astype(jnp.float32)).astype(jnp.bfloat16)
        partial_value = lax.optimization_barrier(partial_value).astype(jnp.float32)
        pair_low = lax.optimization_barrier((partial_value[:, 0] + partial_value[:, 1]).astype(jnp.bfloat16))
        pair_high = lax.optimization_barrier((partial_value[:, 2] + partial_value[:, 3]).astype(jnp.bfloat16))
        return (pair_low.astype(jnp.float32) + pair_high.astype(jnp.float32)).astype(jnp.bfloat16)
    expert_out = lax.map(one_expert, (by_expert, up_stack, down_stack))
    per_block = expert_out.reshape(EXPERTS, blocks, CAP, D).transpose(1, 0, 2, 3).reshape(blocks, EXPERTS * CAP, D)
    routed = jax.vmap(lambda table, index: jnp.take(table, index, axis=0))(per_block, target).reshape(TOKENS, D)
    routed = lax.optimization_barrier(routed).astype(jnp.float32)
    return (activations.astype(jnp.float32) + gate_value[:, None] * routed).astype(jnp.bfloat16)

def reference(carried, norm_gain, router, w_up, w_down, expert_ids):
    upward_list = []
    downward_list = []
    for section_index in range(SECTIONS):
        outputs = [moe_layer(carried[direction, section_index], norm_gain[section_index], router[section_index], w_up[section_index], w_down[section_index], expert_ids[section_index, direction]) for direction in range(2)]
        upward_list.append(outputs[0])
        downward_list.append(outputs[1])
    new_up = jnp.stack([downward_list[0]] + upward_list[:-1])
    new_down = jnp.stack(downward_list[1:] + [upward_list[-1]])
    return jnp.stack([new_up, new_down])
```

```python
import jax
import jax.numpy as jnp
from jax import lax
from jax.experimental import pallas as pl
from jax.experimental.pallas import tpu as pltpu
from jax.sharding import PartitionSpec as P

SPLIT = 4
LANES = 128
MAIN = 8

epsilon = 1e-06
route_scale = 2.5


def iota(shape, dimension):
    return lax.broadcasted_iota(jnp.int32, shape, dimension)


def tail_spread(experts, chunks, padded, back):
    shape = (chunks * experts, experts * padded) if back else (experts * padded, chunks * experts)
    by_expert = iota(shape, 1 if back else 0)
    by_chunk = iota(shape, 0 if back else 1)
    same_expert = by_expert // padded == by_chunk % experts
    same_chunk = by_expert % padded == by_chunk // experts
    return (same_expert & same_chunk).astype(jnp.float32).astype(jnp.bfloat16)


def write_packet(packet_ref, pair, columns):
    experts = packet_ref.shape[0]
    low = columns[:, :LANES].reshape(experts, MAIN, LANES)
    high = columns[:, LANES:].reshape(experts, MAIN, LANES)
    packet_ref[:, pair] = jnp.concatenate([low, high], axis=1).astype(jnp.bfloat16)


def write_tail(packet_ref, stacked):
    experts, blocks = packet_ref.shape[:2]
    pairs = blocks - 2
    spread = tail_spread(experts, 2 * pairs, 32, False)
    tail = jnp.dot(spread, stacked, preferred_element_type=jnp.float32).astype(jnp.bfloat16)
    packet_ref[:, pairs:] = tail.reshape(experts, 2, 16, LANES)


def read_pair(packet_ref, pair):
    experts = packet_ref.shape[0]
    block = packet_ref[:, pair].astype(jnp.float32).reshape(experts, 2, MAIN, LANES)
    low = block[:, 0].reshape(experts * MAIN, LANES)
    high = block[:, 1].reshape(experts * MAIN, LANES)
    return jnp.concatenate([low, high], axis=1).astype(jnp.bfloat16)


def read_tail(packet_ref):
    experts, blocks = packet_ref.shape[:2]
    pairs = blocks - 2
    gather = tail_spread(experts, 2 * pairs, 32, True)
    tail = packet_ref[:, pairs:].reshape(experts * 32, LANES)
    return jnp.dot(gather, tail, preferred_element_type=jnp.float32)


def prepare_kernel(x_ref, gain_ref, router_ref, ids_ref, packet_ref, gate_ref, row_ref):
    experts = packet_ref.shape[0]
    pairs = packet_ref.shape[1] - 2
    tokens = x_ref.shape[2]
    x = x_ref[0, 0].astype(jnp.float32)
    mean_square = jnp.mean(x * x, axis=-1, keepdims=True)
    normed = (x * lax.rsqrt(mean_square + epsilon) * gain_ref[...].astype(jnp.float32)).astype(
        jnp.bfloat16
    )
    logits = jnp.dot(normed, router_ref[0], preferred_element_type=jnp.float32)
    chosen = ids_ref[0, 0]
    one_hot = (iota((tokens, experts), 1) == chosen).astype(jnp.float32)
    gate = route_scale * jax.nn.sigmoid(jnp.sum(logits * one_hot, axis=-1, keepdims=True))
    earlier = (iota((tokens, tokens), 1) < iota((tokens, tokens), 0)).astype(jnp.float32)
    before = jnp.dot(
        earlier.astype(jnp.bfloat16),
        one_hot.astype(jnp.bfloat16),
        preferred_element_type=jnp.float32,
    )
    slot = jnp.sum(before * one_hot, axis=-1, keepdims=True)
    expert = chosen.astype(jnp.float32)
    row = jnp.where(slot < MAIN, expert * MAIN + slot, experts * MAIN + expert)
    gate_ref[...] = jnp.broadcast_to(gate, gate_ref.shape)
    row_ref[...] = jnp.broadcast_to(row, row_ref.shape)
    diagonal = iota((tokens, tokens), 0) == iota((tokens, tokens), 1)
    row_along = jnp.sum(jnp.where(diagonal, row, 0.0), axis=0, keepdims=True)
    rows = experts * (MAIN + 1)
    placer = (iota((rows, tokens), 0).astype(jnp.float32) == row_along).astype(jnp.float32)
    slots = jnp.dot(placer.astype(jnp.bfloat16), normed, preferred_element_type=jnp.float32)
    main, tail = slots[: experts * MAIN], slots[experts * MAIN :]
    for pair in range(pairs):
        write_packet(packet_ref, pair, main[:, pair * 256 : (pair + 1) * 256])
    stacked = jnp.concatenate(
        [tail[:, c * LANES : (c + 1) * LANES] for c in range(2 * pairs)], axis=0
    )
    write_tail(packet_ref, stacked.astype(jnp.bfloat16))


def expert_kernel(own_ref, core_ref, chip_ref, both_ref, up_ref, down_ref, *rest):
    outs, rows_ref = rest[:4], rest[4]
    ins = (own_ref, core_ref, chip_ref, both_ref)
    experts = own_ref.shape[0]
    pairs = own_ref.shape[1] - 2
    main = experts * MAIN
    tails = [read_tail(ref) for ref in ins]
    for pair in range(pairs):
        columns = slice(pair * 256, (pair + 1) * 256)
        for index, ref in enumerate(ins):
            rows_ref[index * main : (index + 1) * main, columns] = read_pair(ref, pair)
        for half in range(2):
            chunk = 2 * pair + half
            block = jnp.concatenate(
                [tail[chunk * experts : (chunk + 1) * experts] for tail in tails], axis=0
            )
            rows_ref[4 * main :, chunk * LANES : (chunk + 1) * LANES] = block.astype(jnp.bfloat16)
    hidden_pre = jnp.dot(rows_ref[...], up_ref[0], preferred_element_type=jnp.float32)
    activated = (hidden_pre / (1.0 + jnp.exp(-hidden_pre))).astype(jnp.bfloat16)
    tail_chunks = [[] for _ in ins]
    for pair in range(pairs):
        columns = slice(pair * 256, (pair + 1) * 256)
        partial = jnp.dot(activated, down_ref[0, :, columns], preferred_element_type=jnp.float32)
        for index, ref in enumerate(outs):
            write_packet(ref, pair, partial[index * main : (index + 1) * main])
            first = 4 * main + index * experts
            for half in range(2):
                tail_chunks[index].append(
                    partial[first : first + experts, half * LANES : (half + 1) * LANES]
                )
    for index, ref in enumerate(outs):
        write_tail(ref, jnp.concatenate(tail_chunks[index], axis=0).astype(jnp.bfloat16))


def finish_kernel(x_ref, packet_ref, gate_ref, row_ref, out_ref):
    experts = packet_ref.shape[0]
    pairs = packet_ref.shape[1] - 2
    tokens = x_ref.shape[2]
    rows = experts * (MAIN + 1)
    row = row_ref[:, :1]
    gate = gate_ref[:, :1]
    chooser = (iota((tokens, rows), 1).astype(jnp.float32) == row).astype(jnp.float32)
    choose_main = chooser[:, : experts * MAIN].astype(jnp.bfloat16)
    choose_tail = chooser[:, experts * MAIN :].astype(jnp.bfloat16)
    tail = read_tail(packet_ref)
    for pair in range(pairs):
        columns = slice(pair * 256, (pair + 1) * 256)
        first = 2 * pair * experts
        tail_pair = jnp.concatenate(
            [tail[first : first + experts], tail[first + experts : first + 2 * experts]], axis=1
        ).astype(jnp.bfloat16)
        routed = jnp.dot(
            choose_main, read_pair(packet_ref, pair), preferred_element_type=jnp.float32
        ) + jnp.dot(choose_tail, tail_pair, preferred_element_type=jnp.float32)
        x = x_ref[0, 0, :, columns].astype(jnp.float32)
        out_ref[:, columns] = (x + gate * routed).astype(jnp.bfloat16)


def params():
    return pltpu.CompilerParams(vmem_limit_bytes=48 * 1024 * 1024)


def whole(array):
    return pl.BlockSpec(array.shape, lambda _: (0,) * array.ndim)


def prepare(direction, carried, gain, router, ids, experts):
    tokens, width = carried.shape[2:]
    blocks = width // 256 + 2
    packet = jax.ShapeDtypeStruct((experts, blocks, 16, LANES), jnp.bfloat16)
    notes = jax.ShapeDtypeStruct((tokens, LANES), jnp.float32)
    return pl.pallas_call(
        prepare_kernel,
        grid=(1,),
        out_shape=(packet, notes, notes),
        in_specs=[
            pl.BlockSpec((1, 1, tokens, width), lambda _: (direction, 0, 0, 0)),
            whole(gain),
            whole(router),
            pl.BlockSpec((1, 1, tokens, 1), lambda _: (0, direction, 0, 0)),
        ],
        out_specs=(whole(packet), whole(notes), whole(notes)),
        compiler_params=params(),
        name="prepare",
    )(carried, gain, router, ids)


def run_expert(own, core, chip, both, up, down):
    experts = own.shape[0]
    packet = jax.ShapeDtypeStruct(own.shape, own.dtype)
    rows = 4 * experts * (MAIN + 1)
    width = up.shape[1]
    return pl.pallas_call(
        expert_kernel,
        grid=(1,),
        out_shape=(packet,) * 4,
        in_specs=[whole(a) for a in (own, core, chip, both, up, down)],
        out_specs=(whole(packet),) * 4,
        scratch_shapes=[pltpu.VMEM((rows, width), jnp.bfloat16)],
        compiler_params=params(),
        name="expert",
    )(own, core, chip, both, up, down)


def finish(direction, carried, packet, gate, row):
    tokens, width = carried.shape[2:]
    out = jax.ShapeDtypeStruct((tokens, width), jnp.bfloat16)
    return pl.pallas_call(
        finish_kernel,
        grid=(1,),
        out_shape=out,
        in_specs=[
            pl.BlockSpec((1, 1, tokens, width), lambda _: (direction, 0, 0, 0)),
            whole(packet),
            whole(gate),
            whole(row),
        ],
        out_specs=whole(out),
        compiler_params=params(),
        name="finish",
    )(carried, packet, gate, row)


def passed_along(block, axis, distance):
    devices = range(lax.axis_size(axis))
    route = [(i - distance, i) for i in devices if i - distance in devices]
    return lax.ppermute(block, axis, route)


def swapped(block, bit):
    return lax.ppermute(
        block, "expert", [(i, i ^ bit) for i in range(lax.axis_size("expert"))]
    )


def exchanged(packet):
    experts = lax.axis_size("expert") // SPLIT
    groups = [[e * SPLIT + k for e in range(experts)] for k in range(SPLIT)]
    return lax.all_to_all(
        packet, "expert", split_axis=0, concat_axis=0, axis_index_groups=groups, tiled=True
    )


def added(left, right):
    return (left.astype(jnp.float32) + right.astype(jnp.float32)).astype(jnp.bfloat16)


def per_device(carried, norm_gain, router, w_up, w_down, expert_ids):
    experts = lax.axis_size("expert") // SPLIT
    layer_outputs = []
    prepared = [
        prepare(direction, carried, norm_gain, router, expert_ids, experts)
        for direction in range(2)
    ]
    for direction in range(2):
        packet, gate, row = prepared[direction]
        own = exchanged(packet)
        chip = swapped(own, 2)
        core = swapped(own, 1)
        both = swapped(chip, 1)
        for_own, for_core, for_chip, for_both = run_expert(own, core, chip, both, w_up, w_down)
        own_sum = added(for_own, swapped(for_core, 1))
        chip_sum = added(for_chip, swapped(for_both, 1))
        total = added(own_sum, swapped(chip_sum, 2))
        returned = exchanged(total)
        layer_outputs.append(finish(direction, carried, returned, gate, row))
    section_index = lax.axis_index("section")
    last_section = lax.axis_size("section") - 1
    from_below = passed_along(layer_outputs[0], "section", 1)
    from_above = passed_along(layer_outputs[1], "section", -1)
    new_up = jnp.where(section_index == 0, layer_outputs[1], from_below)
    new_down = jnp.where(section_index == last_section, layer_outputs[0], from_above)
    return jnp.stack([new_up, new_down])[:, None]


def solution(mesh):
    in_specs = (
        P(None, "section", "expert", None),
        P("section", None),
        P("section", None, None),
        P("section", None, "expert"),
        P("section", "expert", None),
        P("section", None, "expert", None),
    )
    out_specs = P(None, "section", "expert", None)
    return jax.shard_map(
        per_device, mesh=mesh, in_specs=in_specs, out_specs=out_specs, check_vma=False
    )
```

```python
import jax
import jax.numpy as jnp
from jax import lax
from jax.experimental import pallas as pl
from jax.experimental.pallas import tpu as pltpu
from jax.sharding import PartitionSpec as P

SPLIT = 4
LANES = 128
MAIN = 8
PARTS = 2

epsilon = 1e-06
route_scale = 2.5


def iota(shape, dimension):
    return lax.broadcasted_iota(jnp.int32, shape, dimension)


def tail_spread(experts, chunks, padded, back):
    shape = (chunks * experts, experts * padded) if back else (experts * padded, chunks * experts)
    by_expert = iota(shape, 1 if back else 0)
    by_chunk = iota(shape, 0 if back else 1)
    same_expert = by_expert // padded == by_chunk % experts
    same_chunk = by_expert % padded == by_chunk // experts
    return (same_expert & same_chunk).astype(jnp.float32).astype(jnp.bfloat16)


def write_packet(packet_ref, pair, columns):
    experts = packet_ref.shape[0]
    low = columns[:, :LANES].reshape(experts, MAIN, LANES)
    high = columns[:, LANES:].reshape(experts, MAIN, LANES)
    packet_ref[:, pair] = jnp.concatenate([low, high], axis=1).astype(jnp.bfloat16)


def write_tail(packet_ref, stacked):
    experts, blocks = packet_ref.shape[:2]
    pairs = blocks - 2
    spread = tail_spread(experts, 2 * pairs, 32, False)
    tail = jnp.dot(spread, stacked, preferred_element_type=jnp.float32).astype(jnp.bfloat16)
    packet_ref[:, pairs:] = tail.reshape(experts, 2, 16, LANES)


def read_pair(packet_ref, pair):
    experts = packet_ref.shape[0]
    block = packet_ref[:, pair].astype(jnp.float32).reshape(experts, 2, MAIN, LANES)
    low = block[:, 0].reshape(experts * MAIN, LANES)
    high = block[:, 1].reshape(experts * MAIN, LANES)
    return jnp.concatenate([low, high], axis=1).astype(jnp.bfloat16)


def read_tail(packet_ref):
    experts, blocks = packet_ref.shape[:2]
    pairs = blocks - 2
    gather = tail_spread(experts, 2 * pairs, 32, True)
    tail = packet_ref[:, pairs:].reshape(experts * 32, LANES)
    return jnp.dot(gather, tail, preferred_element_type=jnp.float32)


def prepare_kernel(x_ref, gain_ref, router_ref, ids_ref, packets_ref, gate_ref, row_ref):
    for direction in range(x_ref.shape[0]):
        prepare_direction(
            x_ref.at[direction],
            gain_ref,
            router_ref,
            ids_ref.at[0, direction],
            packets_ref.at[:, direction],
            gate_ref.at[direction],
            row_ref.at[direction],
        )


def prepare_direction(x_ref, gain_ref, router_ref, ids_ref, packet_ref, gate_ref, row_ref):
    experts = packet_ref.shape[0]
    pairs = packet_ref.shape[1] - 2
    tokens = x_ref.shape[1]
    x = x_ref[0].astype(jnp.float32)
    mean_square = jnp.mean(x * x, axis=-1, keepdims=True)
    normed = (x * lax.rsqrt(mean_square + epsilon) * gain_ref[...].astype(jnp.float32)).astype(
        jnp.bfloat16
    )
    logits = jnp.dot(normed, router_ref[0], preferred_element_type=jnp.float32)
    chosen = ids_ref[...]
    one_hot = (iota((tokens, experts), 1) == chosen).astype(jnp.float32)
    gate = route_scale * jax.nn.sigmoid(jnp.sum(logits * one_hot, axis=-1, keepdims=True))
    earlier = (iota((tokens, tokens), 1) < iota((tokens, tokens), 0)).astype(jnp.float32)
    before = jnp.dot(
        earlier.astype(jnp.bfloat16),
        one_hot.astype(jnp.bfloat16),
        preferred_element_type=jnp.float32,
    )
    slot = jnp.sum(before * one_hot, axis=-1, keepdims=True)
    expert = chosen.astype(jnp.float32)
    row = jnp.where(slot < MAIN, expert * MAIN + slot, experts * MAIN + expert)
    gate_ref[...] = jnp.broadcast_to(gate, gate_ref.shape)
    row_ref[...] = jnp.broadcast_to(row, row_ref.shape)
    diagonal = iota((tokens, tokens), 0) == iota((tokens, tokens), 1)
    row_along = jnp.sum(jnp.where(diagonal, row, 0.0), axis=0, keepdims=True)
    rows = experts * (MAIN + 1)
    placer = (iota((rows, tokens), 0).astype(jnp.float32) == row_along).astype(jnp.float32)
    slots = jnp.dot(placer.astype(jnp.bfloat16), normed, preferred_element_type=jnp.float32)
    main, tail = slots[: experts * MAIN], slots[experts * MAIN :]
    for pair in range(pairs):
        write_packet(packet_ref, pair, main[:, pair * 256 : (pair + 1) * 256])
    stacked = jnp.concatenate(
        [tail[:, c * LANES : (c + 1) * LANES] for c in range(2 * pairs)], axis=0
    )
    write_tail(packet_ref, stacked.astype(jnp.bfloat16))


def expert_kernel(own_ref, core_ref, chip_ref, both_ref, up_ref, down_ref, *rest):
    outs, rows_ref = rest[:4], rest[4]
    ins = (own_ref, core_ref, chip_ref, both_ref)
    experts = own_ref.shape[0]
    pairs = own_ref.shape[1] - 2
    main = experts * MAIN
    tails = [read_tail(ref) for ref in ins]
    for pair in range(pairs):
        columns = slice(pair * 256, (pair + 1) * 256)
        for index, ref in enumerate(ins):
            rows_ref[index * main : (index + 1) * main, columns] = read_pair(ref, pair)
        for half in range(2):
            chunk = 2 * pair + half
            block = jnp.concatenate(
                [tail[chunk * experts : (chunk + 1) * experts] for tail in tails], axis=0
            )
            rows_ref[4 * main :, chunk * LANES : (chunk + 1) * LANES] = block.astype(jnp.bfloat16)
    hidden_pre = jnp.dot(rows_ref[...], up_ref[0], preferred_element_type=jnp.float32)
    activated = (hidden_pre / (1.0 + jnp.exp(-hidden_pre))).astype(jnp.bfloat16)
    tail_chunks = [[] for _ in ins]
    for pair in range(pairs):
        columns = slice(pair * 256, (pair + 1) * 256)
        partial = jnp.dot(activated, down_ref[0, :, columns], preferred_element_type=jnp.float32)
        for index, ref in enumerate(outs):
            write_packet(ref, pair, partial[index * main : (index + 1) * main])
            first = 4 * main + index * experts
            for half in range(2):
                tail_chunks[index].append(
                    partial[first : first + experts, half * LANES : (half + 1) * LANES]
                )
    for index, ref in enumerate(outs):
        write_tail(ref, jnp.concatenate(tail_chunks[index], axis=0).astype(jnp.bfloat16))


def finish_kernel(x_ref, packets_ref, gate_ref, row_ref, up_ref, down_ref):
    for direction, out_ref in enumerate((up_ref, down_ref)):
        finish_direction(
            x_ref.at[direction],
            packets_ref.at[:, direction],
            gate_ref.at[direction],
            row_ref.at[direction],
            out_ref,
        )


def finish_direction(x_ref, packet_ref, gate_ref, row_ref, out_ref):
    experts = packet_ref.shape[0]
    pairs = packet_ref.shape[1] - 2
    tokens = x_ref.shape[1]
    rows = experts * (MAIN + 1)
    row = row_ref[:, :1]
    gate = gate_ref[:, :1]
    chooser = (iota((tokens, rows), 1).astype(jnp.float32) == row).astype(jnp.float32)
    choose_main = chooser[:, : experts * MAIN].astype(jnp.bfloat16)
    choose_tail = chooser[:, experts * MAIN :].astype(jnp.bfloat16)
    tail = read_tail(packet_ref)
    for pair in range(pairs):
        columns = slice(pair * 256, (pair + 1) * 256)
        first = 2 * pair * experts
        tail_pair = jnp.concatenate(
            [tail[first : first + experts], tail[first + experts : first + 2 * experts]], axis=1
        ).astype(jnp.bfloat16)
        routed = jnp.dot(
            choose_main, read_pair(packet_ref, pair), preferred_element_type=jnp.float32
        ) + jnp.dot(choose_tail, tail_pair, preferred_element_type=jnp.float32)
        x = x_ref[0, :, columns].astype(jnp.float32)
        out_ref[:, columns] = (x + gate * routed).astype(jnp.bfloat16)


def params():
    return pltpu.CompilerParams(vmem_limit_bytes=48 * 1024 * 1024)


def whole(array):
    return pl.BlockSpec(array.shape, lambda _: (0,) * array.ndim)


def prepare(carried, gain, router, ids, experts):
    directions, _, tokens, width = carried.shape
    blocks = width // 256 + 2
    packets = jax.ShapeDtypeStruct((experts, directions, blocks, 16, LANES), jnp.bfloat16)
    notes = jax.ShapeDtypeStruct((directions, tokens, LANES), jnp.float32)
    return pl.pallas_call(
        prepare_kernel,
        grid=(1,),
        out_shape=(packets, notes, notes),
        in_specs=[whole(a) for a in (carried, gain, router, ids)],
        out_specs=(whole(packets), whole(notes), whole(notes)),
        compiler_params=params(),
        name="prepare",
    )(carried, gain, router, ids)


def run_expert(own, core, chip, both, up, down):
    experts = own.shape[0]
    packet = jax.ShapeDtypeStruct(own.shape, own.dtype)
    rows = 4 * experts * (MAIN + 1)
    width = up.shape[1]
    return pl.pallas_call(
        expert_kernel,
        grid=(1,),
        out_shape=(packet,) * 4,
        in_specs=[whole(a) for a in (own, core, chip, both, up, down)],
        out_specs=(whole(packet),) * 4,
        scratch_shapes=[pltpu.VMEM((rows, width), jnp.bfloat16)],
        compiler_params=params(),
        name="expert",
    )(own, core, chip, both, up, down)


def finish(carried, packets, gate, row):
    tokens, width = carried.shape[2:]
    out = jax.ShapeDtypeStruct((tokens, width), jnp.bfloat16)
    return pl.pallas_call(
        finish_kernel,
        grid=(1,),
        out_shape=(out, out),
        in_specs=[whole(a) for a in (carried, packets, gate, row)],
        out_specs=(whole(out), whole(out)),
        compiler_params=params(),
        name="finish",
    )(carried, packets, gate, row)


def passed_along(block, axis, distance):
    devices = range(lax.axis_size(axis))
    route = [(i - distance, i) for i in devices if i - distance in devices]
    return lax.ppermute(block, axis, route)


def swapped(block, bit):
    return lax.ppermute(
        block, "expert", [(i, i ^ bit) for i in range(lax.axis_size("expert"))]
    )


def exchanged(packet):
    experts = lax.axis_size("expert") // SPLIT
    groups = [[e * SPLIT + k for e in range(experts)] for k in range(SPLIT)]
    return lax.all_to_all(
        packet, "expert", split_axis=0, concat_axis=0, axis_index_groups=groups, tiled=True
    )


def added(left, right):
    return (left.astype(jnp.float32) + right.astype(jnp.float32)).astype(jnp.bfloat16)


def per_device(carried, norm_gain, router, w_up, w_down, expert_ids):
    experts = lax.axis_size("expert") // SPLIT
    packets, gate, row = prepare(carried, norm_gain, router, expert_ids, experts)
    received = exchanged(packets)
    peers = experts // PARTS
    totals = []
    for part in range(PARTS):
        own = received[part * peers : (part + 1) * peers].reshape(-1, *packets.shape[2:])
        chip = swapped(own, 2)
        core = swapped(own, 1)
        both = swapped(chip, 1)
        for_own, for_core, for_chip, for_both = run_expert(own, core, chip, both, w_up, w_down)
        own_sum = added(for_own, swapped(for_core, 1))
        chip_sum = added(for_chip, swapped(for_both, 1))
        totals.append(added(own_sum, swapped(chip_sum, 2)).reshape(peers, *packets.shape[1:]))
    returned = exchanged(jnp.concatenate(totals, axis=0))
    layer_outputs = finish(carried, returned, gate, row)
    section_index = lax.axis_index("section")
    last_section = lax.axis_size("section") - 1
    from_below = passed_along(layer_outputs[0], "section", 1)
    from_above = passed_along(layer_outputs[1], "section", -1)
    new_up = jnp.where(section_index == 0, layer_outputs[1], from_below)
    new_down = jnp.where(section_index == last_section, layer_outputs[0], from_above)
    return jnp.stack([new_up, new_down])[:, None]


def solution(mesh):
    in_specs = (
        P(None, "section", "expert", None),
        P("section", None),
        P("section", None, None),
        P("section", None, "expert"),
        P("section", "expert", None),
        P("section", None, "expert", None),
    )
    out_specs = P(None, "section", "expert", None)
    return jax.shard_map(
        per_device, mesh=mesh, in_specs=in_specs, out_specs=out_specs, check_vma=False
    )
```

```python
import jax
import jax.numpy as jnp
from jax import lax
from jax.experimental import pallas as pl
from jax.experimental.pallas import tpu as pltpu
from jax.sharding import PartitionSpec as P

SPLIT = 4
LANES = 128
MAIN = 8

epsilon = 1e-06
route_scale = 2.5

HOPS = (0, 2, 4, 6, -7, -5, -3, -1)
GROUPS = ((2, 5, 3, 4), (0, 7, 1, 6))


def iota(shape, dimension):
    return lax.broadcasted_iota(jnp.int32, shape, dimension)


def tail_spread(experts, chunks, padded, back):
    shape = (chunks * experts, experts * padded) if back else (experts * padded, chunks * experts)
    by_expert = iota(shape, 1 if back else 0)
    by_chunk = iota(shape, 0 if back else 1)
    same_expert = by_expert // padded == by_chunk % experts
    same_chunk = by_expert % padded == by_chunk // experts
    return (same_expert & same_chunk).astype(jnp.float32).astype(jnp.bfloat16)


def write_packet(packet_ref, pair, columns):
    experts = packet_ref.shape[0]
    low = columns[:, :LANES].reshape(experts, MAIN, LANES)
    high = columns[:, LANES:].reshape(experts, MAIN, LANES)
    packet_ref[:, pair] = jnp.concatenate([low, high], axis=1).astype(jnp.bfloat16)


def write_tail(packet_ref, stacked):
    experts, blocks = packet_ref.shape[:2]
    pairs = blocks - 2
    spread = tail_spread(experts, 2 * pairs, 32, False)
    tail = jnp.dot(spread, stacked, preferred_element_type=jnp.float32).astype(jnp.bfloat16)
    packet_ref[:, pairs:] = tail.reshape(experts, 2, 16, LANES)


def read_pair(packet_ref, pair):
    experts = packet_ref.shape[0]
    block = packet_ref[:, pair].astype(jnp.float32).reshape(experts, 2, MAIN, LANES)
    low = block[:, 0].reshape(experts * MAIN, LANES)
    high = block[:, 1].reshape(experts * MAIN, LANES)
    return jnp.concatenate([low, high], axis=1).astype(jnp.bfloat16)


def read_tail(packet_ref):
    experts, blocks = packet_ref.shape[:2]
    pairs = blocks - 2
    gather = tail_spread(experts, 2 * pairs, 32, True)
    tail = packet_ref[:, pairs:].reshape(experts * 32, LANES)
    return jnp.dot(gather, tail, preferred_element_type=jnp.float32)


def prepare_kernel(x_ref, gain_ref, router_ref, ids_ref, turns_ref, gate_ref, row_ref, *packet_refs):
    for direction in range(x_ref.shape[0]):
        prepare_direction(
            x_ref.at[direction],
            gain_ref,
            router_ref,
            ids_ref.at[0, direction],
            turns_ref.at[0, direction],
            gate_ref.at[direction],
            row_ref.at[direction],
            [ref.at[direction] for ref in packet_refs],
        )


def prepare_direction(
    x_ref, gain_ref, router_ref, ids_ref, turns_ref, gate_ref, row_ref, packet_refs
):
    experts = len(packet_refs)
    pairs = packet_refs[0].shape[0] - 2
    tokens = x_ref.shape[1]
    x = x_ref[0].astype(jnp.float32)
    mean_square = jnp.mean(x * x, axis=-1, keepdims=True)
    normed = (x * lax.rsqrt(mean_square + epsilon) * gain_ref[...].astype(jnp.float32)).astype(
        jnp.bfloat16
    )
    logits = jnp.dot(normed, router_ref[0], preferred_element_type=jnp.float32)
    chosen = (iota((tokens, experts), 1) == ids_ref[...]).astype(jnp.float32)
    gate = route_scale * jax.nn.sigmoid(jnp.sum(logits * chosen, axis=-1, keepdims=True))
    turn = turns_ref[...]
    one_hot = (iota((tokens, experts), 1) == turn).astype(jnp.float32)
    earlier = (iota((tokens, tokens), 1) < iota((tokens, tokens), 0)).astype(jnp.float32)
    before = jnp.dot(
        earlier.astype(jnp.bfloat16),
        one_hot.astype(jnp.bfloat16),
        preferred_element_type=jnp.float32,
    )
    slot = jnp.sum(before * one_hot, axis=-1, keepdims=True)
    turn = turn.astype(jnp.float32)
    row = jnp.where(slot < MAIN, turn * MAIN + slot, experts * MAIN + turn)
    gate_ref[...] = jnp.broadcast_to(gate, gate_ref.shape)
    row_ref[...] = jnp.broadcast_to(row, row_ref.shape)
    diagonal = iota((tokens, tokens), 0) == iota((tokens, tokens), 1)
    row_along = jnp.sum(jnp.where(diagonal, row, 0.0), axis=0, keepdims=True)
    rows = experts * (MAIN + 1)
    placer = (iota((rows, tokens), 0).astype(jnp.float32) == row_along).astype(jnp.float32)
    slots = jnp.dot(placer.astype(jnp.bfloat16), normed, preferred_element_type=jnp.float32)
    tail = slots[experts * MAIN :]
    stacked = jnp.concatenate(
        [tail[:, c * LANES : (c + 1) * LANES] for c in range(2 * pairs)], axis=0
    )
    spread = tail_spread(experts, 2 * pairs, 32, False)
    tails = jnp.dot(spread, stacked.astype(jnp.bfloat16), preferred_element_type=jnp.float32)
    for index, packet_ref in enumerate(packet_refs):
        main = slots[index * MAIN : (index + 1) * MAIN]
        for pair in range(pairs):
            first = pair * 256
            block = jnp.concatenate(
                [main[:, first : first + LANES], main[:, first + LANES : first + 256]], axis=0
            )
            packet_ref[pair] = block.astype(jnp.bfloat16)
        last = tails[index * 32 : (index + 1) * 32].astype(jnp.bfloat16)
        packet_ref[pairs:] = last.reshape(2, 16, LANES)


def expert_kernel(own_ref, core_ref, chip_ref, both_ref, up_ref, down_ref, *rest):
    outs, rows_ref = rest[:4], rest[4]
    ins = (own_ref, core_ref, chip_ref, both_ref)
    experts = own_ref.shape[0]
    pairs = own_ref.shape[1] - 2
    main = experts * MAIN
    tails = [read_tail(ref) for ref in ins]
    for pair in range(pairs):
        columns = slice(pair * 256, (pair + 1) * 256)
        for index, ref in enumerate(ins):
            rows_ref[index * main : (index + 1) * main, columns] = read_pair(ref, pair)
        for half in range(2):
            chunk = 2 * pair + half
            block = jnp.concatenate(
                [tail[chunk * experts : (chunk + 1) * experts] for tail in tails], axis=0
            )
            rows_ref[4 * main :, chunk * LANES : (chunk + 1) * LANES] = block.astype(jnp.bfloat16)
    hidden_pre = jnp.dot(rows_ref[...], up_ref[0], preferred_element_type=jnp.float32)
    activated = (hidden_pre / (1.0 + jnp.exp(-hidden_pre))).astype(jnp.bfloat16)
    tail_chunks = [[] for _ in ins]
    for pair in range(pairs):
        columns = slice(pair * 256, (pair + 1) * 256)
        partial = jnp.dot(activated, down_ref[0, :, columns], preferred_element_type=jnp.float32)
        for index, ref in enumerate(outs):
            write_packet(ref, pair, partial[index * main : (index + 1) * main])
            first = 4 * main + index * experts
            for half in range(2):
                tail_chunks[index].append(
                    partial[first : first + experts, half * LANES : (half + 1) * LANES]
                )
    for index, ref in enumerate(outs):
        write_tail(ref, jnp.concatenate(tail_chunks[index], axis=0).astype(jnp.bfloat16))


def finish_kernel(x_ref, gate_ref, row_ref, *rest):
    packet_refs, out_refs = rest[:-2], rest[-2:]
    for direction, out_ref in enumerate(out_refs):
        finish_direction(
            x_ref.at[direction],
            gate_ref.at[direction],
            row_ref.at[direction],
            [ref.at[direction] for ref in packet_refs],
            out_ref,
        )


def finish_direction(x_ref, gate_ref, row_ref, packet_refs, out_ref):
    experts = len(packet_refs)
    pairs = packet_refs[0].shape[0] - 2
    tokens = x_ref.shape[1]
    rows = experts * (MAIN + 1)
    row = row_ref[:, :1]
    gate = gate_ref[:, :1]
    chooser = (iota((tokens, rows), 1).astype(jnp.float32) == row).astype(jnp.float32)
    choose_main = chooser[:, : experts * MAIN].astype(jnp.bfloat16)
    choose_tail = chooser[:, experts * MAIN :].astype(jnp.bfloat16)
    tails = jnp.concatenate([ref[pairs:].reshape(32, LANES) for ref in packet_refs], axis=0)
    gather = tail_spread(experts, 2 * pairs, 32, True)
    tail = jnp.dot(gather, tails, preferred_element_type=jnp.float32)
    for pair in range(pairs):
        columns = slice(pair * 256, (pair + 1) * 256)
        blocks = [ref[pair].astype(jnp.float32) for ref in packet_refs]
        low = jnp.concatenate([block[:MAIN] for block in blocks], axis=0)
        high = jnp.concatenate([block[MAIN:] for block in blocks], axis=0)
        main_pair = jnp.concatenate([low, high], axis=1).astype(jnp.bfloat16)
        first = 2 * pair * experts
        tail_pair = jnp.concatenate(
            [tail[first : first + experts], tail[first + experts : first + 2 * experts]], axis=1
        ).astype(jnp.bfloat16)
        routed = jnp.dot(
            choose_main, main_pair, preferred_element_type=jnp.float32
        ) + jnp.dot(choose_tail, tail_pair, preferred_element_type=jnp.float32)
        x = x_ref[0, :, columns].astype(jnp.float32)
        out_ref[:, columns] = (x + gate * routed).astype(jnp.bfloat16)


def params():
    return pltpu.CompilerParams(vmem_limit_bytes=48 * 1024 * 1024)


def whole(array):
    return pl.BlockSpec(array.shape, lambda _: (0,) * array.ndim)


def prepare(carried, gain, router, ids, turns, experts):
    directions, _, tokens, width = carried.shape
    packet = jax.ShapeDtypeStruct((directions, width // 256 + 2, 16, LANES), jnp.bfloat16)
    notes = jax.ShapeDtypeStruct((directions, tokens, LANES), jnp.float32)
    outs = (notes, notes) + (packet,) * experts
    gate, row, *packets = pl.pallas_call(
        prepare_kernel,
        grid=(1,),
        out_shape=outs,
        in_specs=[whole(a) for a in (carried, gain, router, ids, turns)],
        out_specs=tuple(whole(a) for a in outs),
        compiler_params=params(),
        name="prepare",
    )(carried, gain, router, ids, turns)
    return gate, row, packets


def run_expert(own, core, chip, both, up, down):
    experts = own.shape[0]
    packet = jax.ShapeDtypeStruct(own.shape, own.dtype)
    rows = 4 * experts * (MAIN + 1)
    width = up.shape[1]
    return pl.pallas_call(
        expert_kernel,
        grid=(1,),
        out_shape=(packet,) * 4,
        in_specs=[whole(a) for a in (own, core, chip, both, up, down)],
        out_specs=(whole(packet),) * 4,
        scratch_shapes=[pltpu.VMEM((rows, width), jnp.bfloat16)],
        compiler_params=params(),
        name="expert",
    )(own, core, chip, both, up, down)


def finish(carried, gate, row, packets):
    tokens, width = carried.shape[2:]
    out = jax.ShapeDtypeStruct((tokens, width), jnp.bfloat16)
    operands = (carried, gate, row, *packets)
    return pl.pallas_call(
        finish_kernel,
        grid=(1,),
        out_shape=(out, out),
        in_specs=[whole(a) for a in operands],
        out_specs=(whole(out), whole(out)),
        compiler_params=params(),
        name="finish",
    )(*operands)


def passed_along(block, axis, distance):
    devices = range(lax.axis_size(axis))
    route = [(i - distance, i) for i in devices if i - distance in devices]
    return lax.ppermute(block, axis, route)


def swapped(block, bit):
    return lax.ppermute(
        block, "expert", [(i, i ^ bit) for i in range(lax.axis_size("expert"))]
    )


def delivered(packet, turn, back):
    if HOPS[turn] == 0:
        return packet
    devices = lax.axis_size("expert")
    route = []
    for device in range(devices):
        chips = HOPS[turn] if device // 2 % 2 == 0 else -HOPS[turn]
        there = (device + 2 * chips) % devices
        route.append((there, device) if back else (device, there))
    return lax.ppermute(packet, "expert", route)


def added(left, right):
    return (left.astype(jnp.float32) + right.astype(jnp.float32)).astype(jnp.bfloat16)


def per_device(carried, norm_gain, router, w_up, w_down, expert_ids):
    experts = lax.axis_size("expert") // SPLIT
    device = lax.axis_index("expert")
    pair = device // SPLIT
    lower = device // 2 % 2 == 0
    turns = jnp.where(lower, expert_ids - pair, pair - expert_ids) % experts
    gate, row, packets = prepare(carried, norm_gain, router, expert_ids, turns, experts)
    arrived = [delivered(packet, turn, False) for turn, packet in enumerate(packets)]
    returned = [None] * experts
    for group in GROUPS:
        own = jnp.concatenate([arrived[turn] for turn in group], axis=0)
        chip = swapped(own, 2)
        core = swapped(own, 1)
        both = swapped(chip, 1)
        for_own, for_core, for_chip, for_both = run_expert(own, core, chip, both, w_up, w_down)
        own_sum = added(for_own, swapped(for_core, 1))
        chip_sum = added(for_chip, swapped(for_both, 1))
        from_chip = swapped(chip_sum, 2)
        for place, turn in enumerate(group):
            part = slice(2 * place, 2 * place + 2)
            returned[turn] = delivered(added(own_sum[part], from_chip[part]), turn, True)
    layer_outputs = finish(carried, gate, row, returned)
    section_index = lax.axis_index("section")
    last_section = lax.axis_size("section") - 1
    from_below = passed_along(layer_outputs[0], "section", 1)
    from_above = passed_along(layer_outputs[1], "section", -1)
    new_up = jnp.where(section_index == 0, layer_outputs[1], from_below)
    new_down = jnp.where(section_index == last_section, layer_outputs[0], from_above)
    return jnp.stack([new_up, new_down])[:, None]


def solution(mesh):
    in_specs = (
        P(None, "section", "expert", None),
        P("section", None),
        P("section", None, None),
        P("section", None, "expert"),
        P("section", "expert", None),
        P("section", None, "expert", None),
    )
    out_specs = P(None, "section", "expert", None)
    return jax.shard_map(
        per_device, mesh=mesh, in_specs=in_specs, out_specs=out_specs, check_vma=False
    )
```

```python
import jax
import jax.numpy as jnp
from jax import lax
from jax.experimental import pallas as pl
from jax.experimental.pallas import tpu as pltpu
from jax.sharding import PartitionSpec as P

SPLIT = 4
LANES = 128
MAIN = 8

epsilon = 1e-06
route_scale = 2.5

HOPS = (0, 2, 4, 6, -7, -5, -3, -1)
GROUPS = ((2, 5, 3, 4), (0, 7, 1, 6))


def iota(shape, dimension):
    return lax.broadcasted_iota(jnp.int32, shape, dimension)


def tail_spread(experts, chunks, padded, back):
    shape = (chunks * experts, experts * padded) if back else (experts * padded, chunks * experts)
    by_expert = iota(shape, 1 if back else 0)
    by_chunk = iota(shape, 0 if back else 1)
    same_expert = by_expert // padded == by_chunk % experts
    same_chunk = by_expert % padded == by_chunk // experts
    return (same_expert & same_chunk).astype(jnp.float32).astype(jnp.bfloat16)


def write_packet(packet_ref, pair, columns):
    experts = packet_ref.shape[0]
    low = columns[:, :LANES].reshape(experts, MAIN, LANES)
    high = columns[:, LANES:].reshape(experts, MAIN, LANES)
    packet_ref[:, pair] = jnp.concatenate([low, high], axis=1).astype(jnp.bfloat16)


def write_tail(packet_ref, stacked):
    experts, blocks = packet_ref.shape[:2]
    pairs = blocks - 2
    spread = tail_spread(experts, 2 * pairs, 32, False)
    tail = jnp.dot(spread, stacked, preferred_element_type=jnp.float32).astype(jnp.bfloat16)
    packet_ref[:, pairs:] = tail.reshape(experts, 2, 16, LANES)


def read_pair(packet_ref, pair):
    experts = packet_ref.shape[0]
    block = packet_ref[:, pair].astype(jnp.float32).reshape(experts, 2, MAIN, LANES)
    low = block[:, 0].reshape(experts * MAIN, LANES)
    high = block[:, 1].reshape(experts * MAIN, LANES)
    return jnp.concatenate([low, high], axis=1).astype(jnp.bfloat16)


def read_tail(packet_ref):
    experts, blocks = packet_ref.shape[:2]
    pairs = blocks - 2
    gather = tail_spread(experts, 2 * pairs, 32, True)
    tail = packet_ref[:, pairs:].reshape(experts * 32, LANES)
    return jnp.dot(gather, tail, preferred_element_type=jnp.float32)


def prepare_kernel(x_ref, gain_ref, router_ref, ids_ref, turns_ref, gate_ref, row_ref, *packet_refs):
    for direction in range(x_ref.shape[0]):
        prepare_direction(
            x_ref.at[direction],
            gain_ref,
            router_ref,
            ids_ref.at[0, direction],
            turns_ref.at[0, direction],
            gate_ref.at[direction],
            row_ref.at[direction],
            [ref.at[direction] for ref in packet_refs],
        )


def prepare_direction(
    x_ref, gain_ref, router_ref, ids_ref, turns_ref, gate_ref, row_ref, packet_refs
):
    experts = len(packet_refs)
    pairs = packet_refs[0].shape[0] - 2
    tokens = x_ref.shape[1]
    x = x_ref[0].astype(jnp.float32)
    mean_square = jnp.mean(x * x, axis=-1, keepdims=True)
    normed = (x * lax.rsqrt(mean_square + epsilon) * gain_ref[...].astype(jnp.float32)).astype(
        jnp.bfloat16
    )
    logits = jnp.dot(normed, router_ref[0], preferred_element_type=jnp.float32)
    chosen = (iota((tokens, experts), 1) == ids_ref[...]).astype(jnp.float32)
    gate = route_scale * jax.nn.sigmoid(jnp.sum(logits * chosen, axis=-1, keepdims=True))
    turn = turns_ref[...]
    one_hot = (iota((tokens, experts), 1) == turn).astype(jnp.float32)
    earlier = (iota((tokens, tokens), 1) < iota((tokens, tokens), 0)).astype(jnp.float32)
    before = jnp.dot(
        earlier.astype(jnp.bfloat16),
        one_hot.astype(jnp.bfloat16),
        preferred_element_type=jnp.float32,
    )
    slot = jnp.sum(before * one_hot, axis=-1, keepdims=True)
    turn = turn.astype(jnp.float32)
    row = jnp.where(slot < MAIN, turn * MAIN + slot, experts * MAIN + turn)
    gate_ref[...] = jnp.broadcast_to(gate, gate_ref.shape)
    row_ref[...] = jnp.broadcast_to(row, row_ref.shape)
    diagonal = iota((tokens, tokens), 0) == iota((tokens, tokens), 1)
    row_along = jnp.sum(jnp.where(diagonal, row, 0.0), axis=0, keepdims=True)
    rows = experts * (MAIN + 1)
    placer = (iota((rows, tokens), 0).astype(jnp.float32) == row_along).astype(jnp.float32)
    slots = jnp.dot(placer.astype(jnp.bfloat16), normed, preferred_element_type=jnp.float32)
    tail = slots[experts * MAIN :]
    stacked = jnp.concatenate(
        [tail[:, c * LANES : (c + 1) * LANES] for c in range(2 * pairs)], axis=0
    )
    spread = tail_spread(experts, 2 * pairs, 32, False)
    tails = jnp.dot(spread, stacked.astype(jnp.bfloat16), preferred_element_type=jnp.float32)
    for index, packet_ref in enumerate(packet_refs):
        main = slots[index * MAIN : (index + 1) * MAIN]
        for pair in range(pairs):
            first = pair * 256
            block = jnp.concatenate(
                [main[:, first : first + LANES], main[:, first + LANES : first + 256]], axis=0
            )
            packet_ref[pair] = block.astype(jnp.bfloat16)
        last = tails[index * 32 : (index + 1) * 32].astype(jnp.bfloat16)
        packet_ref[pairs:] = last.reshape(2, 16, LANES)


def expert_kernel(own_ref, chip_ref, *rest):
    ups, downs, outs, rows_ref = rest[:2], rest[2:4], rest[4:6], rest[6]
    ins = (own_ref, chip_ref)
    packets = own_ref.shape[0]
    pairs = own_ref.shape[1] - 2
    main = packets * MAIN
    tails = [read_tail(ref) for ref in ins]
    for pair in range(pairs):
        columns = slice(pair * 256, (pair + 1) * 256)
        for index, ref in enumerate(ins):
            rows_ref[index * main : (index + 1) * main, columns] = read_pair(ref, pair)
        for half in range(2):
            chunk = 2 * pair + half
            block = jnp.concatenate(
                [tail[chunk * packets : (chunk + 1) * packets] for tail in tails], axis=0
            )
            rows_ref[2 * main :, chunk * LANES : (chunk + 1) * LANES] = block.astype(jnp.bfloat16)
    rows = rows_ref[...]
    activated = []
    for up_ref in ups:
        hidden_pre = jnp.dot(rows, up_ref[0], preferred_element_type=jnp.float32)
        activated.append((hidden_pre / (1.0 + jnp.exp(-hidden_pre))).astype(jnp.bfloat16))
    tail_chunks = [[] for _ in ins]
    for pair in range(pairs):
        columns = slice(pair * 256, (pair + 1) * 256)
        partial = sum(
            jnp.dot(part, down_ref[0, :, columns], preferred_element_type=jnp.float32)
            for part, down_ref in zip(activated, downs)
        )
        for index, ref in enumerate(outs):
            write_packet(ref, pair, partial[index * main : (index + 1) * main])
            first = 2 * main + index * packets
            for half in range(2):
                tail_chunks[index].append(
                    partial[first : first + packets, half * LANES : (half + 1) * LANES]
                )
    for index, ref in enumerate(outs):
        write_tail(ref, jnp.concatenate(tail_chunks[index], axis=0).astype(jnp.bfloat16))


def finish_kernel(x_ref, gate_ref, row_ref, *rest):
    packet_refs, out_refs = rest[:-2], rest[-2:]
    for direction, out_ref in enumerate(out_refs):
        finish_direction(
            x_ref.at[direction],
            gate_ref.at[direction],
            row_ref.at[direction],
            [ref.at[direction] for ref in packet_refs],
            out_ref,
        )


def finish_direction(x_ref, gate_ref, row_ref, packet_refs, out_ref):
    experts = len(packet_refs)
    pairs = packet_refs[0].shape[0] - 2
    tokens = x_ref.shape[1]
    rows = experts * (MAIN + 1)
    row = row_ref[:, :1]
    gate = gate_ref[:, :1]
    chooser = (iota((tokens, rows), 1).astype(jnp.float32) == row).astype(jnp.float32)
    choose_main = chooser[:, : experts * MAIN].astype(jnp.bfloat16)
    choose_tail = chooser[:, experts * MAIN :].astype(jnp.bfloat16)
    tails = jnp.concatenate([ref[pairs:].reshape(32, LANES) for ref in packet_refs], axis=0)
    gather = tail_spread(experts, 2 * pairs, 32, True)
    tail = jnp.dot(gather, tails, preferred_element_type=jnp.float32)
    for pair in range(pairs):
        columns = slice(pair * 256, (pair + 1) * 256)
        blocks = [ref[pair].astype(jnp.float32) for ref in packet_refs]
        low = jnp.concatenate([block[:MAIN] for block in blocks], axis=0)
        high = jnp.concatenate([block[MAIN:] for block in blocks], axis=0)
        main_pair = jnp.concatenate([low, high], axis=1).astype(jnp.bfloat16)
        first = 2 * pair * experts
        tail_pair = jnp.concatenate(
            [tail[first : first + experts], tail[first + experts : first + 2 * experts]], axis=1
        ).astype(jnp.bfloat16)
        routed = jnp.dot(
            choose_main, main_pair, preferred_element_type=jnp.float32
        ) + jnp.dot(choose_tail, tail_pair, preferred_element_type=jnp.float32)
        x = x_ref[0, :, columns].astype(jnp.float32)
        out_ref[:, columns] = (x + gate * routed).astype(jnp.bfloat16)


def params():
    return pltpu.CompilerParams(vmem_limit_bytes=48 * 1024 * 1024)


def whole(array):
    return pl.BlockSpec(array.shape, lambda _: (0,) * array.ndim)


def prepare(carried, gain, router, ids, turns, experts):
    directions, _, tokens, width = carried.shape
    packet = jax.ShapeDtypeStruct((directions, width // 256 + 2, 16, LANES), jnp.bfloat16)
    notes = jax.ShapeDtypeStruct((directions, tokens, LANES), jnp.float32)
    outs = (notes, notes) + (packet,) * experts
    gate, row, *packets = pl.pallas_call(
        prepare_kernel,
        grid=(1,),
        out_shape=outs,
        in_specs=[whole(a) for a in (carried, gain, router, ids, turns)],
        out_specs=tuple(whole(a) for a in outs),
        compiler_params=params(),
        name="prepare",
    )(carried, gain, router, ids, turns)
    return gate, row, packets


def run_expert(own, chip, ups, downs):
    packet = jax.ShapeDtypeStruct(own.shape, own.dtype)
    rows = 2 * own.shape[0] * (MAIN + 1)
    width = ups[0].shape[1]
    operands = (own, chip, *ups, *downs)
    return pl.pallas_call(
        expert_kernel,
        grid=(1,),
        out_shape=(packet,) * 2,
        in_specs=[whole(a) for a in operands],
        out_specs=(whole(packet),) * 2,
        scratch_shapes=[pltpu.VMEM((rows, width), jnp.bfloat16)],
        compiler_params=params(),
        name="expert",
    )(*operands)


def finish(carried, gate, row, packets):
    tokens, width = carried.shape[2:]
    out = jax.ShapeDtypeStruct((tokens, width), jnp.bfloat16)
    operands = (carried, gate, row, *packets)
    return pl.pallas_call(
        finish_kernel,
        grid=(1,),
        out_shape=(out, out),
        in_specs=[whole(a) for a in operands],
        out_specs=(whole(out), whole(out)),
        compiler_params=params(),
        name="finish",
    )(*operands)


def passed_along(block, axis, distance):
    devices = range(lax.axis_size(axis))
    route = [(i - distance, i) for i in devices if i - distance in devices]
    return lax.ppermute(block, axis, route)


def swapped(block, bit):
    return lax.ppermute(
        block, "expert", [(i, i ^ bit) for i in range(lax.axis_size("expert"))]
    )


def delivered(packet, turn, back):
    if HOPS[turn] == 0:
        return packet
    devices = lax.axis_size("expert")
    route = []
    for device in range(devices):
        chips = HOPS[turn] if device // 2 % 2 == 0 else -HOPS[turn]
        there = (device + 2 * chips) % devices
        route.append((there, device) if back else (device, there))
    return lax.ppermute(packet, "expert", route)


def added(left, right):
    return (left.astype(jnp.float32) + right.astype(jnp.float32)).astype(jnp.bfloat16)


def per_device(carried, norm_gain, router, w_up, w_down, expert_ids):
    experts = lax.axis_size("expert") // SPLIT
    device = lax.axis_index("expert")
    pair = device // SPLIT
    lower = device // 2 % 2 == 0
    turns = jnp.where(lower, expert_ids - pair, pair - expert_ids) % experts
    gate, row, packets = prepare(carried, norm_gain, router, expert_ids, turns, experts)
    arrived = [delivered(packet, turn, False) for turn, packet in enumerate(packets)]
    returned = [None] * experts
    ups = (w_up, swapped(w_up, 1))
    downs = (w_down, swapped(w_down, 1))
    for group in GROUPS:
        own = jnp.concatenate([arrived[turn] for turn in group], axis=0)
        for_own, for_chip = run_expert(own, swapped(own, 2), ups, downs)
        from_chip = swapped(for_chip, 2)
        for place, turn in enumerate(group):
            part = slice(2 * place, 2 * place + 2)
            returned[turn] = delivered(added(for_own[part], from_chip[part]), turn, True)
    layer_outputs = finish(carried, gate, row, returned)
    section_index = lax.axis_index("section")
    last_section = lax.axis_size("section") - 1
    from_below = passed_along(layer_outputs[0], "section", 1)
    from_above = passed_along(layer_outputs[1], "section", -1)
    new_up = jnp.where(section_index == 0, layer_outputs[1], from_below)
    new_down = jnp.where(section_index == last_section, layer_outputs[0], from_above)
    return jnp.stack([new_up, new_down])[:, None]


def solution(mesh):
    in_specs = (
        P(None, "section", "expert", None),
        P("section", None),
        P("section", None, None),
        P("section", None, "expert"),
        P("section", "expert", None),
        P("section", None, "expert", None),
    )
    out_specs = P(None, "section", "expert", None)
    return jax.shard_map(
        per_device, mesh=mesh, in_specs=in_specs, out_specs=out_specs, check_vma=False
    )
```

```python
import jax
import jax.numpy as jnp
from jax import lax
from jax.experimental import pallas as pl
from jax.experimental.pallas import tpu as pltpu
from jax.sharding import PartitionSpec as P

SPLIT = 4
LANES = 128
MAIN = 8

epsilon = 1e-06
route_scale = 2.5

HOPS = (0, 2, 4, 6, -7, -5, -3, -1)
GROUPS = ((2, 5, 3, 4), (0, 7, 1, 6))


def iota(shape, dimension):
    return lax.broadcasted_iota(jnp.int32, shape, dimension)


def tail_spread(experts, chunks, padded, back):
    shape = (chunks * experts, experts * padded) if back else (experts * padded, chunks * experts)
    by_expert = iota(shape, 1 if back else 0)
    by_chunk = iota(shape, 0 if back else 1)
    same_expert = by_expert // padded == by_chunk % experts
    same_chunk = by_expert % padded == by_chunk // experts
    return (same_expert & same_chunk).astype(jnp.float32).astype(jnp.bfloat16)


def write_packet(packet_ref, pair, columns):
    experts = packet_ref.shape[0]
    low = columns[:, :LANES].reshape(experts, MAIN, LANES)
    high = columns[:, LANES:].reshape(experts, MAIN, LANES)
    packet_ref[:, pair] = jnp.concatenate([low, high], axis=1).astype(jnp.bfloat16)


def write_tail(packet_ref, stacked):
    experts, blocks = packet_ref.shape[:2]
    pairs = blocks - 2
    spread = tail_spread(experts, 2 * pairs, 32, False)
    tail = jnp.dot(spread, stacked, preferred_element_type=jnp.float32).astype(jnp.bfloat16)
    packet_ref[:, pairs:] = tail.reshape(experts, 2, 16, LANES)


def read_pair(packet_ref, pair):
    experts = packet_ref.shape[0]
    block = packet_ref[:, pair].astype(jnp.float32).reshape(experts, 2, MAIN, LANES)
    low = block[:, 0].reshape(experts * MAIN, LANES)
    high = block[:, 1].reshape(experts * MAIN, LANES)
    return jnp.concatenate([low, high], axis=1).astype(jnp.bfloat16)


def read_tail(packet_ref):
    experts, blocks = packet_ref.shape[:2]
    pairs = blocks - 2
    gather = tail_spread(experts, 2 * pairs, 32, True)
    tail = packet_ref[:, pairs:].reshape(experts * 32, LANES)
    return jnp.dot(gather, tail, preferred_element_type=jnp.float32)


def column(along):
    count = along.shape[1]
    diagonal = iota((count, count), 0) == iota((count, count), 1)
    return jnp.sum(jnp.where(diagonal, along, 0.0), axis=1, keepdims=True)


def prepare_kernel(x_ref, gain_ref, router_ref, ids_ref, gate_ref, row_ref, *packet_refs):
    for direction in range(x_ref.shape[0]):
        prepare_direction(
            x_ref.at[direction, 0],
            gain_ref,
            router_ref,
            ids_ref.at[0, direction],
            gate_ref.at[direction],
            row_ref.at[direction],
            [ref.at[direction] for ref in packet_refs],
        )


def prepare_direction(x_ref, gain_ref, router_ref, ids_ref, gate_ref, row_ref, packet_refs):
    experts = len(packet_refs)
    pairs = packet_refs[0].shape[0] - 2
    tokens = x_ref.shape[0]
    x = x_ref[...].astype(jnp.float32)
    mean_square = jnp.mean(x * x, axis=-1, keepdims=True)
    normed = (x * lax.rsqrt(mean_square + epsilon) * gain_ref[...].astype(jnp.float32)).astype(
        jnp.bfloat16
    )
    logits = lax.dot_general(
        normed, router_ref[0], (((1,), (1,)), ((), ())), preferred_element_type=jnp.float32
    )
    expert = column(ids_ref[...].astype(jnp.float32))
    by_expert = iota((tokens, experts), 1).astype(jnp.float32)
    chosen = (by_expert == expert).astype(jnp.float32)
    gate = route_scale * jax.nn.sigmoid(jnp.sum(logits * chosen, axis=-1, keepdims=True))
    device = lax.axis_index("expert")
    home = (device // SPLIT).astype(jnp.float32)
    turn = jnp.where(device // 2 % 2 == 0, expert - home, home - expert)
    turn = jnp.where(turn < 0.0, turn + experts, turn)
    one_hot = (by_expert == turn).astype(jnp.float32)
    earlier = (iota((tokens, tokens), 1) < iota((tokens, tokens), 0)).astype(jnp.float32)
    before = jnp.dot(
        earlier.astype(jnp.bfloat16),
        one_hot.astype(jnp.bfloat16),
        preferred_element_type=jnp.float32,
    )
    slot = jnp.sum(before * one_hot, axis=-1, keepdims=True)
    row = jnp.where(slot < MAIN, turn * MAIN + slot, experts * MAIN + turn)
    gate_ref[...] = jnp.broadcast_to(gate, gate_ref.shape)
    row_ref[...] = jnp.broadcast_to(row, row_ref.shape)
    diagonal = iota((tokens, tokens), 0) == iota((tokens, tokens), 1)
    row_along = jnp.sum(jnp.where(diagonal, row, 0.0), axis=0, keepdims=True)
    rows = experts * (MAIN + 1)
    placer = (iota((rows, tokens), 0).astype(jnp.float32) == row_along).astype(jnp.float32)
    slots = jnp.dot(placer.astype(jnp.bfloat16), normed, preferred_element_type=jnp.float32)
    tail = slots[experts * MAIN :]
    stacked = jnp.concatenate(
        [tail[:, c * LANES : (c + 1) * LANES] for c in range(2 * pairs)], axis=0
    )
    spread = tail_spread(experts, 2 * pairs, 32, False)
    tails = jnp.dot(spread, stacked.astype(jnp.bfloat16), preferred_element_type=jnp.float32)
    for index, packet_ref in enumerate(packet_refs):
        main = slots[index * MAIN : (index + 1) * MAIN]
        for pair in range(pairs):
            first = pair * 256
            block = jnp.concatenate(
                [main[:, first : first + LANES], main[:, first + LANES : first + 256]], axis=0
            )
            packet_ref[pair] = block.astype(jnp.bfloat16)
        last = tails[index * 32 : (index + 1) * 32].astype(jnp.bfloat16)
        packet_ref[pairs:] = last.reshape(2, 16, LANES)


def expert_kernel(own_ref, chip_ref, *rest):
    ups, downs, outs, rows_ref = rest[:2], rest[2:4], rest[4:6], rest[6]
    ins = (own_ref, chip_ref)
    packets = own_ref.shape[0]
    pairs = own_ref.shape[1] - 2
    main = packets * MAIN
    tails = [read_tail(ref) for ref in ins]
    for pair in range(pairs):
        columns = slice(pair * 256, (pair + 1) * 256)
        for index, ref in enumerate(ins):
            rows_ref[index * main : (index + 1) * main, columns] = read_pair(ref, pair)
        for half in range(2):
            chunk = 2 * pair + half
            block = jnp.concatenate(
                [tail[chunk * packets : (chunk + 1) * packets] for tail in tails], axis=0
            )
            rows_ref[2 * main :, chunk * LANES : (chunk + 1) * LANES] = block.astype(jnp.bfloat16)
    rows = rows_ref[...]
    activated = []
    for up_ref in ups:
        hidden_pre = jnp.dot(rows, up_ref[0], preferred_element_type=jnp.float32)
        activated.append((hidden_pre / (1.0 + jnp.exp(-hidden_pre))).astype(jnp.bfloat16))
    tail_chunks = [[] for _ in ins]
    for pair in range(pairs):
        columns = slice(pair * 256, (pair + 1) * 256)
        partial = sum(
            jnp.dot(part, down_ref[0, :, columns], preferred_element_type=jnp.float32)
            for part, down_ref in zip(activated, downs)
        )
        for index, ref in enumerate(outs):
            write_packet(ref, pair, partial[index * main : (index + 1) * main])
            first = 2 * main + index * packets
            for half in range(2):
                tail_chunks[index].append(
                    partial[first : first + packets, half * LANES : (half + 1) * LANES]
                )
    for index, ref in enumerate(outs):
        write_tail(ref, jnp.concatenate(tail_chunks[index], axis=0).astype(jnp.bfloat16))


def finish_kernel(x_ref, gate_ref, row_ref, *rest):
    packet_refs, out_refs = rest[:-2], rest[-2:]
    for direction, out_ref in enumerate(out_refs):
        finish_direction(
            x_ref.at[direction],
            gate_ref.at[direction],
            row_ref.at[direction],
            [ref.at[direction] for ref in packet_refs],
            out_ref,
        )


def finish_direction(x_ref, gate_ref, row_ref, packet_refs, out_ref):
    experts = len(packet_refs)
    pairs = packet_refs[0].shape[0] - 2
    tokens = x_ref.shape[1]
    rows = experts * (MAIN + 1)
    row = row_ref[:, :1]
    gate = gate_ref[:, :1]
    chooser = (iota((tokens, rows), 1).astype(jnp.float32) == row).astype(jnp.float32)
    choose_main = chooser[:, : experts * MAIN].astype(jnp.bfloat16)
    choose_tail = chooser[:, experts * MAIN :].astype(jnp.bfloat16)
    tails = jnp.concatenate([ref[pairs:].reshape(32, LANES) for ref in packet_refs], axis=0)
    gather = tail_spread(experts, 2 * pairs, 32, True)
    tail = jnp.dot(gather, tails, preferred_element_type=jnp.float32)
    for pair in range(pairs):
        columns = slice(pair * 256, (pair + 1) * 256)
        blocks = [ref[pair].astype(jnp.float32) for ref in packet_refs]
        low = jnp.concatenate([block[:MAIN] for block in blocks], axis=0)
        high = jnp.concatenate([block[MAIN:] for block in blocks], axis=0)
        main_pair = jnp.concatenate([low, high], axis=1).astype(jnp.bfloat16)
        first = 2 * pair * experts
        tail_pair = jnp.concatenate(
            [tail[first : first + experts], tail[first + experts : first + 2 * experts]], axis=1
        ).astype(jnp.bfloat16)
        routed = jnp.dot(
            choose_main, main_pair, preferred_element_type=jnp.float32
        ) + jnp.dot(choose_tail, tail_pair, preferred_element_type=jnp.float32)
        x = x_ref[0, :, columns].astype(jnp.float32)
        out_ref[:, columns] = (x + gate * routed).astype(jnp.bfloat16)


def params():
    return pltpu.CompilerParams(vmem_limit_bytes=48 * 1024 * 1024)


def whole(array):
    return pl.BlockSpec(array.shape, lambda _: (0,) * array.ndim)


def prepare(carried, gain, router, ids, experts):
    directions, _, tokens, width = carried.shape
    packet = jax.ShapeDtypeStruct((directions, width // 256 + 2, 16, LANES), jnp.bfloat16)
    notes = jax.ShapeDtypeStruct((directions, tokens, LANES), jnp.float32)
    outs = (notes, notes) + (packet,) * experts
    operands = (carried, gain, jnp.swapaxes(router, 1, 2), jnp.swapaxes(ids, 2, 3))
    gate, row, *packets = pl.pallas_call(
        prepare_kernel,
        grid=(1,),
        out_shape=outs,
        in_specs=[whole(a) for a in operands],
        out_specs=tuple(whole(a) for a in outs),
        compiler_params=params(),
        name="prepare",
    )(*operands)
    return gate, row, packets


def run_expert(own, chip, ups, downs):
    packet = jax.ShapeDtypeStruct(own.shape, own.dtype)
    rows = 2 * own.shape[0] * (MAIN + 1)
    width = ups[0].shape[1]
    operands = (own, chip, *ups, *downs)
    return pl.pallas_call(
        expert_kernel,
        grid=(1,),
        out_shape=(packet,) * 2,
        in_specs=[whole(a) for a in operands],
        out_specs=(whole(packet),) * 2,
        scratch_shapes=[pltpu.VMEM((rows, width), jnp.bfloat16)],
        compiler_params=params(),
        name="expert",
    )(*operands)


def finish(carried, gate, row, packets):
    tokens, width = carried.shape[2:]
    out = jax.ShapeDtypeStruct((tokens, width), jnp.bfloat16)
    operands = (carried, gate, row, *packets)
    return pl.pallas_call(
        finish_kernel,
        grid=(1,),
        out_shape=(out, out),
        in_specs=[whole(a) for a in operands],
        out_specs=(whole(out), whole(out)),
        compiler_params=params(),
        name="finish",
    )(*operands)


def passed_along(block, axis, distance):
    devices = range(lax.axis_size(axis))
    route = [(i - distance, i) for i in devices if i - distance in devices]
    return lax.ppermute(block, axis, route)


def swapped(block, bit):
    return lax.ppermute(
        block, "expert", [(i, i ^ bit) for i in range(lax.axis_size("expert"))]
    )


def delivered(packet, turn, back):
    if HOPS[turn] == 0:
        return packet
    devices = lax.axis_size("expert")
    route = []
    for device in range(devices):
        chips = HOPS[turn] if device // 2 % 2 == 0 else -HOPS[turn]
        there = (device + 2 * chips) % devices
        route.append((there, device) if back else (device, there))
    return lax.ppermute(packet, "expert", route)


def added(left, right):
    return (left.astype(jnp.float32) + right.astype(jnp.float32)).astype(jnp.bfloat16)


def after(value, *earlier):
    return lax.optimization_barrier((value, *earlier))[0]


def per_device(carried, norm_gain, router, w_up, w_down, expert_ids):
    experts = lax.axis_size("expert") // SPLIT
    ups = (w_up, swapped(w_up, 1))
    downs = (w_down, swapped(w_down, 1))
    gate, row, packets = prepare(carried, norm_gain, router, expert_ids, experts)
    packets = [after(packet, ups[1], downs[1]) for packet in packets]
    arrived = [delivered(packet, turn, False) for turn, packet in enumerate(packets)]
    returned = [None] * experts
    for group in GROUPS:
        own = jnp.concatenate([arrived[turn] for turn in group], axis=0)
        for_own, for_chip = run_expert(own, swapped(own, 2), ups, downs)
        from_chip = swapped(for_chip, 2)
        for place, turn in enumerate(group):
            part = slice(2 * place, 2 * place + 2)
            returned[turn] = delivered(added(for_own[part], from_chip[part]), turn, True)
    layer_outputs = finish(carried, gate, row, returned)
    section_index = lax.axis_index("section")
    last_section = lax.axis_size("section") - 1
    from_below = passed_along(layer_outputs[0], "section", 1)
    from_above = passed_along(layer_outputs[1], "section", -1)
    new_up = jnp.where(section_index == 0, layer_outputs[1], from_below)
    new_down = jnp.where(section_index == last_section, layer_outputs[0], from_above)
    return jnp.stack([new_up, new_down])[:, None]


def solution(mesh):
    in_specs = (
        P(None, "section", "expert", None),
        P("section", None),
        P("section", None, None),
        P("section", None, "expert"),
        P("section", "expert", None),
        P("section", None, "expert", None),
    )
    out_specs = P(None, "section", "expert", None)
    return jax.shard_map(
        per_device, mesh=mesh, in_specs=in_specs, out_specs=out_specs, check_vma=False
    )
```

```python
import jax
import jax.numpy as jnp
from jax import lax
from jax.experimental import pallas as pl
from jax.experimental.pallas import tpu as pltpu
from jax.sharding import PartitionSpec as P

SPLIT = 4
LANES = 128
MAIN = 8

epsilon = 1e-06
route_scale = 2.5

HOPS = (0, 2, 4, 6, -7, -5, -3, -1)
GROUPS = ((2, 5, 3, 4), (0, 7, 1, 6))


def iota(shape, dimension):
    return lax.broadcasted_iota(jnp.int32, shape, dimension)


def tail_spread(experts, chunks, padded, back):
    shape = (chunks * experts, experts * padded) if back else (experts * padded, chunks * experts)
    by_expert = iota(shape, 1 if back else 0)
    by_chunk = iota(shape, 0 if back else 1)
    same_expert = by_expert // padded == by_chunk % experts
    same_chunk = by_expert % padded == by_chunk // experts
    return (same_expert & same_chunk).astype(jnp.float32).astype(jnp.bfloat16)


def write_packet(packet_ref, pair, columns):
    experts = packet_ref.shape[0]
    low = columns[:, :LANES].reshape(experts, MAIN, LANES)
    high = columns[:, LANES:].reshape(experts, MAIN, LANES)
    packet_ref[:, pair] = jnp.concatenate([low, high], axis=1).astype(jnp.bfloat16)


def write_tail(packet_ref, stacked):
    experts, blocks = packet_ref.shape[:2]
    pairs = blocks - 2
    spread = tail_spread(experts, 2 * pairs, 32, False)
    tail = jnp.dot(spread, stacked, preferred_element_type=jnp.float32).astype(jnp.bfloat16)
    packet_ref[:, pairs:] = tail.reshape(experts, 2, 16, LANES)


def read_pair(packet_ref, pair):
    experts = packet_ref.shape[0]
    block = packet_ref[:, pair].astype(jnp.float32).reshape(experts, 2, MAIN, LANES)
    low = block[:, 0].reshape(experts * MAIN, LANES)
    high = block[:, 1].reshape(experts * MAIN, LANES)
    return jnp.concatenate([low, high], axis=1).astype(jnp.bfloat16)


def read_tail(packet_ref):
    experts, blocks = packet_ref.shape[:2]
    pairs = blocks - 2
    gather = tail_spread(experts, 2 * pairs, 32, True)
    tail = packet_ref[:, pairs:].reshape(experts * 32, LANES)
    return jnp.dot(gather, tail, preferred_element_type=jnp.float32)


def column(along):
    count = along.shape[1]
    diagonal = iota((count, count), 0) == iota((count, count), 1)
    return jnp.sum(jnp.where(diagonal, along, 0.0), axis=1, keepdims=True)


def prepare_kernel(x_ref, gain_ref, router_ref, ids_ref, gate_ref, row_ref, *packet_refs):
    for direction in range(x_ref.shape[0]):
        prepare_direction(
            x_ref.at[direction, 0],
            gain_ref,
            router_ref,
            ids_ref.at[0, direction],
            gate_ref.at[direction],
            row_ref.at[direction],
            [ref.at[direction] for ref in packet_refs],
        )


def prepare_direction(x_ref, gain_ref, router_ref, ids_ref, gate_ref, row_ref, packet_refs):
    experts = len(packet_refs)
    pairs = packet_refs[0].shape[0] - 2
    tokens = x_ref.shape[0]
    x = x_ref[...].astype(jnp.float32)
    mean_square = jnp.mean(x * x, axis=-1, keepdims=True)
    normed = (x * lax.rsqrt(mean_square + epsilon) * gain_ref[...].astype(jnp.float32)).astype(
        jnp.bfloat16
    )
    logits = lax.dot_general(
        normed, router_ref[0], (((1,), (1,)), ((), ())), preferred_element_type=jnp.float32
    )
    expert = column(ids_ref[...].astype(jnp.float32))
    by_expert = iota((tokens, experts), 1).astype(jnp.float32)
    chosen = (by_expert == expert).astype(jnp.float32)
    gate = route_scale * jax.nn.sigmoid(jnp.sum(logits * chosen, axis=-1, keepdims=True))
    device = lax.axis_index("expert")
    home = (device // SPLIT).astype(jnp.float32)
    turn = jnp.where(device // 2 % 2 == 0, expert - home, home - expert)
    turn = jnp.where(turn < 0.0, turn + experts, turn)
    one_hot = (by_expert == turn).astype(jnp.float32)
    earlier = (iota((tokens, tokens), 1) < iota((tokens, tokens), 0)).astype(jnp.float32)
    before = jnp.dot(
        earlier.astype(jnp.bfloat16),
        one_hot.astype(jnp.bfloat16),
        preferred_element_type=jnp.float32,
    )
    slot = jnp.sum(before * one_hot, axis=-1, keepdims=True)
    row = jnp.where(slot < MAIN, turn * MAIN + slot, experts * MAIN + turn)
    gate_ref[...] = jnp.broadcast_to(gate, gate_ref.shape)
    row_ref[...] = jnp.broadcast_to(row, row_ref.shape)
    diagonal = iota((tokens, tokens), 0) == iota((tokens, tokens), 1)
    row_along = jnp.sum(jnp.where(diagonal, row, 0.0), axis=0, keepdims=True)
    rows = experts * (MAIN + 1)
    placer = (iota((rows, tokens), 0).astype(jnp.float32) == row_along).astype(jnp.float32)
    slots = jnp.dot(placer.astype(jnp.bfloat16), normed, preferred_element_type=jnp.float32)
    tail = slots[experts * MAIN :]
    stacked = jnp.concatenate(
        [tail[:, c * LANES : (c + 1) * LANES] for c in range(2 * pairs)], axis=0
    )
    spread = tail_spread(experts, 2 * pairs, 32, False)
    tails = jnp.dot(spread, stacked.astype(jnp.bfloat16), preferred_element_type=jnp.float32)
    for index, packet_ref in enumerate(packet_refs):
        main = slots[index * MAIN : (index + 1) * MAIN]
        for pair in range(pairs):
            first = pair * 256
            block = jnp.concatenate(
                [main[:, first : first + LANES], main[:, first + LANES : first + 256]], axis=0
            )
            packet_ref[pair] = block.astype(jnp.bfloat16)
        last = tails[index * 32 : (index + 1) * 32].astype(jnp.bfloat16)
        packet_ref[pairs:] = last.reshape(2, 16, LANES)


def expert_kernel(own_ref, chip_ref, *rest):
    ups, down_sources, outs, downs, arrived = rest[:2], rest[2:4], rest[4:6], rest[6:8], rest[8]
    copies = [
        pltpu.make_async_copy(source, down_ref, arrived.at[core])
        for core, (source, down_ref) in enumerate(zip(down_sources, downs))
    ]
    for copy in copies:
        copy.start()
    ins = (own_ref, chip_ref)
    packets = own_ref.shape[0]
    pairs = own_ref.shape[1] - 2
    main = packets * MAIN
    tails = [read_tail(ref) for ref in ins]
    hidden_pre = [0.0, 0.0]
    for pair in range(pairs):
        first = 2 * pair * packets
        low = [tail[first : first + packets] for tail in tails]
        high = [tail[first + packets : first + 2 * packets] for tail in tails]
        last = jnp.concatenate(
            [jnp.concatenate(low, axis=0), jnp.concatenate(high, axis=0)], axis=1
        )
        rows = jnp.concatenate(
            [read_pair(ref, pair) for ref in ins] + [last.astype(jnp.bfloat16)], axis=0
        )
        for core, up_ref in enumerate(ups):
            hidden_pre[core] = hidden_pre[core] + jnp.dot(
                rows, up_ref[0, pair * 256 : (pair + 1) * 256], preferred_element_type=jnp.float32
            )
    activated = [
        (hidden / (1.0 + jnp.exp(-hidden))).astype(jnp.bfloat16) for hidden in hidden_pre
    ]
    for copy in copies:
        copy.wait()
    tail_chunks = [[] for _ in ins]
    for pair in range(pairs):
        columns = slice(pair * 256, (pair + 1) * 256)
        partial = sum(
            jnp.dot(part, down_ref[0, :, columns], preferred_element_type=jnp.float32)
            for part, down_ref in zip(activated, downs)
        )
        for index, ref in enumerate(outs):
            write_packet(ref, pair, partial[index * main : (index + 1) * main])
            first = 2 * main + index * packets
            for half in range(2):
                tail_chunks[index].append(
                    partial[first : first + packets, half * LANES : (half + 1) * LANES]
                )
    for index, ref in enumerate(outs):
        write_tail(ref, jnp.concatenate(tail_chunks[index], axis=0).astype(jnp.bfloat16))


def finish_kernel(x_ref, gate_ref, row_ref, *rest):
    packet_refs, out_refs = rest[:-2], rest[-2:]
    for direction, out_ref in enumerate(out_refs):
        finish_direction(
            x_ref.at[direction],
            gate_ref.at[direction],
            row_ref.at[direction],
            [ref.at[direction] for ref in packet_refs],
            out_ref,
        )


def finish_direction(x_ref, gate_ref, row_ref, packet_refs, out_ref):
    experts = len(packet_refs)
    pairs = packet_refs[0].shape[0] - 2
    tokens = x_ref.shape[1]
    rows = experts * (MAIN + 1)
    row = row_ref[:, :1]
    gate = gate_ref[:, :1]
    chooser = (iota((tokens, rows), 1).astype(jnp.float32) == row).astype(jnp.float32)
    choose_main = chooser[:, : experts * MAIN].astype(jnp.bfloat16)
    choose_tail = chooser[:, experts * MAIN :].astype(jnp.bfloat16)
    tails = jnp.concatenate([ref[pairs:].reshape(32, LANES) for ref in packet_refs], axis=0)
    gather = tail_spread(experts, 2 * pairs, 32, True)
    tail = jnp.dot(gather, tails, preferred_element_type=jnp.float32)
    for pair in range(pairs):
        columns = slice(pair * 256, (pair + 1) * 256)
        blocks = [ref[pair].astype(jnp.float32) for ref in packet_refs]
        low = jnp.concatenate([block[:MAIN] for block in blocks], axis=0)
        high = jnp.concatenate([block[MAIN:] for block in blocks], axis=0)
        main_pair = jnp.concatenate([low, high], axis=1).astype(jnp.bfloat16)
        first = 2 * pair * experts
        tail_pair = jnp.concatenate(
            [tail[first : first + experts], tail[first + experts : first + 2 * experts]], axis=1
        ).astype(jnp.bfloat16)
        routed = jnp.dot(
            choose_main, main_pair, preferred_element_type=jnp.float32
        ) + jnp.dot(choose_tail, tail_pair, preferred_element_type=jnp.float32)
        x = x_ref[0, :, columns].astype(jnp.float32)
        out_ref[:, columns] = (x + gate * routed).astype(jnp.bfloat16)


def params():
    return pltpu.CompilerParams(vmem_limit_bytes=48 * 1024 * 1024)


def whole(array):
    return pl.BlockSpec(array.shape, lambda _: (0,) * array.ndim)


def prepare(carried, gain, router, ids, experts):
    directions, _, tokens, width = carried.shape
    packet = jax.ShapeDtypeStruct((directions, width // 256 + 2, 16, LANES), jnp.bfloat16)
    notes = jax.ShapeDtypeStruct((directions, tokens, LANES), jnp.float32)
    outs = (notes, notes) + (packet,) * experts
    operands = (carried, gain, jnp.swapaxes(router, 1, 2), jnp.swapaxes(ids, 2, 3))
    gate, row, *packets = pl.pallas_call(
        prepare_kernel,
        grid=(1,),
        out_shape=outs,
        in_specs=[whole(a) for a in operands],
        out_specs=tuple(whole(a) for a in outs),
        compiler_params=params(),
        name="prepare",
    )(*operands)
    return gate, row, packets


def run_expert(own, chip, ups, downs):
    packet = jax.ShapeDtypeStruct(own.shape, own.dtype)
    operands = (own, chip, *ups, *downs)
    return pl.pallas_call(
        expert_kernel,
        grid=(1,),
        out_shape=(packet,) * 2,
        in_specs=[whole(a) for a in (own, chip, *ups)]
        + [pl.BlockSpec(memory_space=pl.ANY) for _ in downs],
        out_specs=(whole(packet),) * 2,
        scratch_shapes=[pltpu.VMEM(a.shape, a.dtype) for a in downs]
        + [pltpu.SemaphoreType.DMA((len(downs),))],
        compiler_params=params(),
        name="expert",
    )(*operands)


def finish(carried, gate, row, packets):
    tokens, width = carried.shape[2:]
    out = jax.ShapeDtypeStruct((tokens, width), jnp.bfloat16)
    operands = (carried, gate, row, *packets)
    return pl.pallas_call(
        finish_kernel,
        grid=(1,),
        out_shape=(out, out),
        in_specs=[whole(a) for a in operands],
        out_specs=(whole(out), whole(out)),
        compiler_params=params(),
        name="finish",
    )(*operands)


def passed_along(block, axis, distance):
    devices = range(lax.axis_size(axis))
    route = [(i - distance, i) for i in devices if i - distance in devices]
    return lax.ppermute(block, axis, route)


def swapped(block, bit):
    return lax.ppermute(
        block, "expert", [(i, i ^ bit) for i in range(lax.axis_size("expert"))]
    )


def delivered(packet, turn, back):
    if HOPS[turn] == 0:
        return packet
    devices = lax.axis_size("expert")
    route = []
    for device in range(devices):
        chips = HOPS[turn] if device // 2 % 2 == 0 else -HOPS[turn]
        there = (device + 2 * chips) % devices
        route.append((there, device) if back else (device, there))
    return lax.ppermute(packet, "expert", route)


def added(left, right):
    return (left.astype(jnp.float32) + right.astype(jnp.float32)).astype(jnp.bfloat16)


def after(value, *earlier):
    return lax.optimization_barrier((value, *earlier))[0]


def per_device(carried, norm_gain, router, w_up, w_down, expert_ids):
    experts = lax.axis_size("expert") // SPLIT
    ups = (w_up, swapped(w_up, 1))
    downs = (w_down, swapped(w_down, 1))
    gate, row, packets = prepare(carried, norm_gain, router, expert_ids, experts)
    packets = [after(packet, ups[1], downs[1]) for packet in packets]
    arrived = [delivered(packet, turn, False) for turn, packet in enumerate(packets)]
    returned = [None] * experts
    for group in GROUPS:
        own = jnp.concatenate([arrived[turn] for turn in group], axis=0)
        for_own, for_chip = run_expert(own, swapped(own, 2), ups, downs)
        from_chip = swapped(for_chip, 2)
        for place, turn in enumerate(group):
            part = slice(2 * place, 2 * place + 2)
            returned[turn] = delivered(added(for_own[part], from_chip[part]), turn, True)
    layer_outputs = finish(carried, gate, row, returned)
    section_index = lax.axis_index("section")
    last_section = lax.axis_size("section") - 1
    from_below = passed_along(layer_outputs[0], "section", 1)
    from_above = passed_along(layer_outputs[1], "section", -1)
    new_up = jnp.where(section_index == 0, layer_outputs[1], from_below)
    new_down = jnp.where(section_index == last_section, layer_outputs[0], from_above)
    return jnp.stack([new_up, new_down])[:, None]


def solution(mesh):
    in_specs = (
        P(None, "section", "expert", None),
        P("section", None),
        P("section", None, None),
        P("section", None, "expert"),
        P("section", "expert", None),
        P("section", None, "expert", None),
    )
    out_specs = P(None, "section", "expert", None)
    return jax.shard_map(
        per_device, mesh=mesh, in_specs=in_specs, out_specs=out_specs, check_vma=False
    )
```

```python
import functools

import jax
import jax.numpy as jnp
from jax import lax
from jax.experimental import pallas as pl
from jax.experimental.pallas import tpu as pltpu
from jax.sharding import PartitionSpec as P

SPLIT = 4
LANES = 128
MAIN = 8

epsilon = 1e-06
route_scale = 2.5

HOPS = (0, 2, 4, 6, -7, -5, -3, -1)
GROUPS = ((2, 5, 3, 4), (0, 7, 1, 6))


def iota(shape, dimension):
    return lax.broadcasted_iota(jnp.int32, shape, dimension)


def tail_spread(experts, chunks, padded, back):
    shape = (chunks * experts, experts * padded) if back else (experts * padded, chunks * experts)
    by_expert = iota(shape, 1 if back else 0)
    by_chunk = iota(shape, 0 if back else 1)
    same_expert = by_expert // padded == by_chunk % experts
    same_chunk = by_expert % padded == by_chunk // experts
    return (same_expert & same_chunk).astype(jnp.float32).astype(jnp.bfloat16)


def write_packet(packet_ref, pair, columns):
    experts = packet_ref.shape[0]
    low = columns[:, :LANES].reshape(experts, MAIN, LANES)
    high = columns[:, LANES:].reshape(experts, MAIN, LANES)
    packet_ref[:, pair] = jnp.concatenate([low, high], axis=1).astype(jnp.bfloat16)


def write_tail(packet_ref, stacked):
    experts, blocks = packet_ref.shape[:2]
    pairs = blocks - 2
    spread = tail_spread(experts, 2 * pairs, 32, False)
    tail = jnp.dot(spread, stacked, preferred_element_type=jnp.float32).astype(jnp.bfloat16)
    packet_ref[:, pairs:] = tail.reshape(experts, 2, 16, LANES)


def read_pair(packet_ref, pair):
    experts = packet_ref.shape[0]
    block = packet_ref[:, pair].astype(jnp.float32).reshape(experts, 2, MAIN, LANES)
    low = block[:, 0].reshape(experts * MAIN, LANES)
    high = block[:, 1].reshape(experts * MAIN, LANES)
    return jnp.concatenate([low, high], axis=1).astype(jnp.bfloat16)


def read_tail(packet_ref):
    experts, blocks = packet_ref.shape[:2]
    pairs = blocks - 2
    gather = tail_spread(experts, 2 * pairs, 32, True)
    tail = packet_ref[:, pairs:].reshape(experts * 32, LANES)
    return jnp.dot(gather, tail, preferred_element_type=jnp.float32)


def column(along):
    count = along.shape[1]
    diagonal = iota((count, count), 0) == iota((count, count), 1)
    return jnp.sum(jnp.where(diagonal, along, 0.0), axis=1, keepdims=True)


def prepare_kernel(x_ref, gain_ref, router_ref, ids_ref, gate_ref, row_ref, *packet_refs):
    for direction in range(x_ref.shape[0]):
        prepare_direction(
            x_ref.at[direction, 0],
            gain_ref,
            router_ref,
            ids_ref.at[0, direction],
            gate_ref.at[direction],
            row_ref.at[direction],
            [ref.at[direction] for ref in packet_refs],
        )


def prepare_direction(x_ref, gain_ref, router_ref, ids_ref, gate_ref, row_ref, packet_refs):
    experts = len(packet_refs)
    pairs = packet_refs[0].shape[0] - 2
    tokens = x_ref.shape[0]
    x = x_ref[...].astype(jnp.float32)
    mean_square = jnp.mean(x * x, axis=-1, keepdims=True)
    normed = (x * lax.rsqrt(mean_square + epsilon) * gain_ref[...].astype(jnp.float32)).astype(
        jnp.bfloat16
    )
    logits = lax.dot_general(
        normed, router_ref[0], (((1,), (1,)), ((), ())), preferred_element_type=jnp.float32
    )
    expert = column(ids_ref[...].astype(jnp.float32))
    by_expert = iota((tokens, experts), 1).astype(jnp.float32)
    chosen = (by_expert == expert).astype(jnp.float32)
    gate = route_scale * jax.nn.sigmoid(jnp.sum(logits * chosen, axis=-1, keepdims=True))
    device = lax.axis_index("expert")
    home = (device // SPLIT).astype(jnp.float32)
    turn = jnp.where(device // 2 % 2 == 0, expert - home, home - expert)
    turn = jnp.where(turn < 0.0, turn + experts, turn)
    one_hot = (by_expert == turn).astype(jnp.float32)
    earlier = (iota((tokens, tokens), 1) < iota((tokens, tokens), 0)).astype(jnp.float32)
    before = jnp.dot(
        earlier.astype(jnp.bfloat16),
        one_hot.astype(jnp.bfloat16),
        preferred_element_type=jnp.float32,
    )
    slot = jnp.sum(before * one_hot, axis=-1, keepdims=True)
    row = jnp.where(slot < MAIN, turn * MAIN + slot, experts * MAIN + turn)
    gate_ref[...] = jnp.broadcast_to(gate, gate_ref.shape)
    row_ref[...] = jnp.broadcast_to(row, row_ref.shape)
    diagonal = iota((tokens, tokens), 0) == iota((tokens, tokens), 1)
    row_along = jnp.sum(jnp.where(diagonal, row, 0.0), axis=0, keepdims=True)
    rows = experts * (MAIN + 1)
    placer = (iota((rows, tokens), 0).astype(jnp.float32) == row_along).astype(jnp.float32)
    slots = jnp.dot(placer.astype(jnp.bfloat16), normed, preferred_element_type=jnp.float32)
    tail = slots[experts * MAIN :]
    stacked = jnp.concatenate(
        [tail[:, c * LANES : (c + 1) * LANES] for c in range(2 * pairs)], axis=0
    )
    spread = tail_spread(experts, 2 * pairs, 32, False)
    tails = jnp.dot(spread, stacked.astype(jnp.bfloat16), preferred_element_type=jnp.float32)
    for index, packet_ref in enumerate(packet_refs):
        main = slots[index * MAIN : (index + 1) * MAIN]
        for pair in range(pairs):
            first = pair * 256
            block = jnp.concatenate(
                [main[:, first : first + LANES], main[:, first + LANES : first + 256]], axis=0
            )
            packet_ref[pair] = block.astype(jnp.bfloat16)
        last = tails[index * 32 : (index + 1) * 32].astype(jnp.bfloat16)
        packet_ref[pairs:] = last.reshape(2, 16, LANES)


def expert_kernel(own_ref, chip_ref, *rest):
    ups, down_sources, outs, downs, arrived = rest[:2], rest[2:4], rest[4:6], rest[6:8], rest[8]
    copies = [
        pltpu.make_async_copy(source, down_ref, arrived.at[core])
        for core, (source, down_ref) in enumerate(zip(down_sources, downs))
    ]
    for copy in copies:
        copy.start()
    ins = (own_ref, chip_ref)
    packets = own_ref.shape[0]
    pairs = own_ref.shape[1] - 2
    main = packets * MAIN
    tails = [read_tail(ref) for ref in ins]
    hidden_pre = [0.0, 0.0]
    for pair in range(pairs):
        first = 2 * pair * packets
        low = [tail[first : first + packets] for tail in tails]
        high = [tail[first + packets : first + 2 * packets] for tail in tails]
        last = jnp.concatenate(
            [jnp.concatenate(low, axis=0), jnp.concatenate(high, axis=0)], axis=1
        )
        rows = jnp.concatenate(
            [read_pair(ref, pair) for ref in ins] + [last.astype(jnp.bfloat16)], axis=0
        )
        for core, up_ref in enumerate(ups):
            hidden_pre[core] = hidden_pre[core] + jnp.dot(
                rows, up_ref[0, pair * 256 : (pair + 1) * 256], preferred_element_type=jnp.float32
            )
    activated = [
        (hidden / (1.0 + jnp.exp(-hidden))).astype(jnp.bfloat16) for hidden in hidden_pre
    ]
    for copy in copies:
        copy.wait()
    tail_chunks = [[] for _ in ins]
    for pair in range(pairs):
        columns = slice(pair * 256, (pair + 1) * 256)
        partial = sum(
            jnp.dot(part, down_ref[0, :, columns], preferred_element_type=jnp.float32)
            for part, down_ref in zip(activated, downs)
        )
        for index, ref in enumerate(outs):
            write_packet(ref, pair, partial[index * main : (index + 1) * main])
            first = 2 * main + index * packets
            for half in range(2):
                tail_chunks[index].append(
                    partial[first : first + packets, half * LANES : (half + 1) * LANES]
                )
    for index, ref in enumerate(outs):
        write_tail(ref, jnp.concatenate(tail_chunks[index], axis=0).astype(jnp.bfloat16))


def finish_kernel(direction, x_ref, gate_ref, row_ref, *rest):
    finish_direction(
        x_ref.at[direction],
        gate_ref.at[direction],
        row_ref.at[direction],
        [ref.at[direction] for ref in rest[:-1]],
        rest[-1],
    )


def finish_direction(x_ref, gate_ref, row_ref, packet_refs, out_ref):
    experts = len(packet_refs)
    pairs = packet_refs[0].shape[0] - 2
    tokens = x_ref.shape[1]
    rows = experts * (MAIN + 1)
    row = row_ref[:, :1]
    gate = gate_ref[:, :1]
    chooser = (iota((tokens, rows), 1).astype(jnp.float32) == row).astype(jnp.float32)
    choose_main = chooser[:, : experts * MAIN].astype(jnp.bfloat16)
    choose_tail = chooser[:, experts * MAIN :].astype(jnp.bfloat16)
    tails = jnp.concatenate([ref[pairs:].reshape(32, LANES) for ref in packet_refs], axis=0)
    gather = tail_spread(experts, 2 * pairs, 32, True)
    tail = jnp.dot(gather, tails, preferred_element_type=jnp.float32)
    for pair in range(pairs):
        columns = slice(pair * 256, (pair + 1) * 256)
        blocks = [ref[pair].astype(jnp.float32) for ref in packet_refs]
        low = jnp.concatenate([block[:MAIN] for block in blocks], axis=0)
        high = jnp.concatenate([block[MAIN:] for block in blocks], axis=0)
        main_pair = jnp.concatenate([low, high], axis=1).astype(jnp.bfloat16)
        first = 2 * pair * experts
        tail_pair = jnp.concatenate(
            [tail[first : first + experts], tail[first + experts : first + 2 * experts]], axis=1
        ).astype(jnp.bfloat16)
        routed = jnp.dot(
            choose_main, main_pair, preferred_element_type=jnp.float32
        ) + jnp.dot(choose_tail, tail_pair, preferred_element_type=jnp.float32)
        x = x_ref[0, :, columns].astype(jnp.float32)
        out_ref[:, columns] = (x + gate * routed).astype(jnp.bfloat16)


def params():
    return pltpu.CompilerParams(vmem_limit_bytes=48 * 1024 * 1024)


def whole(array):
    return pl.BlockSpec(array.shape, lambda _: (0,) * array.ndim)


def prepare(carried, gain, router, ids, experts):
    directions, _, tokens, width = carried.shape
    packet = jax.ShapeDtypeStruct((directions, width // 256 + 2, 16, LANES), jnp.bfloat16)
    notes = jax.ShapeDtypeStruct((directions, tokens, LANES), jnp.float32)
    outs = (notes, notes) + (packet,) * experts
    operands = (carried, gain, jnp.swapaxes(router, 1, 2), jnp.swapaxes(ids, 2, 3))
    gate, row, *packets = pl.pallas_call(
        prepare_kernel,
        grid=(1,),
        out_shape=outs,
        in_specs=[whole(a) for a in operands],
        out_specs=tuple(whole(a) for a in outs),
        compiler_params=params(),
        name="prepare",
    )(*operands)
    return gate, row, packets


def run_expert(own, chip, ups, downs):
    packet = jax.ShapeDtypeStruct(own.shape, own.dtype)
    operands = (own, chip, *ups, *downs)
    return pl.pallas_call(
        expert_kernel,
        grid=(1,),
        out_shape=(packet,) * 2,
        in_specs=[whole(a) for a in (own, chip, *ups)]
        + [pl.BlockSpec(memory_space=pl.ANY) for _ in downs],
        out_specs=(whole(packet),) * 2,
        scratch_shapes=[pltpu.VMEM(a.shape, a.dtype) for a in downs]
        + [pltpu.SemaphoreType.DMA((len(downs),))],
        compiler_params=params(),
        name="expert",
    )(*operands)


def finish(direction, carried, gate, row, packets):
    tokens, width = carried.shape[2:]
    out = jax.ShapeDtypeStruct((tokens, width), jnp.bfloat16)
    operands = (carried, gate, row, *packets)
    return pl.pallas_call(
        functools.partial(finish_kernel, direction),
        grid=(1,),
        out_shape=out,
        in_specs=[whole(a) for a in operands],
        out_specs=whole(out),
        compiler_params=params(),
        name="finish",
    )(*operands)


def passed_along(block, axis, distance):
    devices = range(lax.axis_size(axis))
    route = [(i - distance, i) for i in devices if i - distance in devices]
    return lax.ppermute(block, axis, route)


def swapped(block, bit):
    return lax.ppermute(
        block, "expert", [(i, i ^ bit) for i in range(lax.axis_size("expert"))]
    )


def delivered(packet, turn, back):
    if HOPS[turn] == 0:
        return packet
    devices = lax.axis_size("expert")
    route = []
    for device in range(devices):
        chips = HOPS[turn] if device // 2 % 2 == 0 else -HOPS[turn]
        there = (device + 2 * chips) % devices
        route.append((there, device) if back else (device, there))
    return lax.ppermute(packet, "expert", route)


def added(left, right):
    return (left.astype(jnp.float32) + right.astype(jnp.float32)).astype(jnp.bfloat16)


def after(value, *earlier):
    return lax.optimization_barrier((value, *earlier))[0]


def per_device(carried, norm_gain, router, w_up, w_down, expert_ids):
    experts = lax.axis_size("expert") // SPLIT
    ups = (w_up, swapped(w_up, 1))
    downs = (w_down, swapped(w_down, 1))
    gate, row, packets = prepare(carried, norm_gain, router, expert_ids, experts)
    packets = [after(packet, ups[1], downs[1]) for packet in packets]
    arrived = [delivered(packet, turn, False) for turn, packet in enumerate(packets)]
    returned = [None] * experts
    for group in GROUPS:
        own = jnp.concatenate([arrived[turn] for turn in group], axis=0)
        for_own, for_chip = run_expert(own, swapped(own, 2), ups, downs)
        from_chip = swapped(for_chip, 2)
        for place, turn in enumerate(group):
            part = slice(2 * place, 2 * place + 2)
            returned[turn] = delivered(added(for_own[part], from_chip[part]), turn, True)
    layer_outputs = [finish(d, carried, gate, row, returned) for d in range(2)]
    section_index = lax.axis_index("section")
    last_section = lax.axis_size("section") - 1
    from_below = passed_along(layer_outputs[0], "section", 1)
    from_above = passed_along(layer_outputs[1], "section", -1)
    new_up = jnp.where(section_index == 0, layer_outputs[1], from_below)
    new_down = jnp.where(section_index == last_section, layer_outputs[0], from_above)
    return jnp.stack([new_up, new_down])[:, None]


def solution(mesh):
    in_specs = (
        P(None, "section", "expert", None),
        P("section", None),
        P("section", None, None),
        P("section", None, "expert"),
        P("section", "expert", None),
        P("section", None, "expert", None),
    )
    out_specs = P(None, "section", "expert", None)
    return jax.shard_map(
        per_device, mesh=mesh, in_specs=in_specs, out_specs=out_specs, check_vma=False
    )
```
